32 devices in a mesh: ctx: 16 (over z, x, core), head: 2 (over y).
Axes of the slice: x: 2, y: 2, z: 4, core: 2. Of those that a mesh axis runs over, the one named last changes fastest.
Arguments:
- queries: bfloat16 [4096, 2048], P('ctx', 'head'), as said below
- keys: bfloat16 [4096, 2048], P('ctx', 'head'), as said below
- values: bfloat16 [4096, 2048], P('ctx', 'head'), may hold values from -6 to 6
- dout: bfloat16 [4096, 2048], P('ctx', 'head'), may hold values from -6 to 6
- beacon_keys: bfloat16 [512, 2048], P('ctx', 'head'), may hold values from -6 to 6
- beacon_values: bfloat16 [512, 2048], P('ctx', 'head'), may hold values from -6 to 6
- beacon_key_weight: bfloat16 [4096, 2048], P('ctx', 'head'), may hold values from -0.125 to 0.125
- beacon_value_weight: bfloat16 [4096, 2048], P('ctx', 'head'), may hold values from -0.125 to 0.125
- lengths: int32 [16], replicated, may hold values from 1 to 256, as said below
- counts: int32 [16], replicated, may hold values from 1 to 32, as said below
Outputs:
- query_grad: bfloat16 [4096, 2048], P('ctx', 'head')
- key_grad: bfloat16 [4096, 2048], P('ctx', 'head')
- value_grad: bfloat16 [4096, 2048], P('ctx', 'head')
- beacon_key_grad: bfloat16 [512, 2048], P('ctx', 'head')
- beacon_value_grad: bfloat16 [512, 2048], P('ctx', 'head')
- beacon_hidden_grad: bfloat16 [512, 4096], P('ctx', 'head')
The draws below stay inside these ranges and needn't reach their ends.
Inputs may be any that keep to these rules, and one draw needn't show every extreme that they name: `queries`: every entry lies in -10 to 10. `keys`: every entry lies in -10 to 10. `lengths`: some group has exactly 256 raw tokens in every draw. counts[c] = ceil(lengths[c] / 8).
All inputs are finite; a program needn't handle non-finite values.
Results may differ from the reference program's by a relative error of at most 0.019.
Values may be sent and summed in bfloat16 or wider, within the bound.
A program may use at most 64 MiB of HBM per device.

```python
import jax
import jax.numpy as jnp
from jax import lax

D = 4096
HEADS = 16
HEAD_DIM = 128
RATIO = 8
GROUP = 256
BEACON = 32
TOKENS = 4096
BEACONS = 512
N_CTX = 16


def token_lengths(key):
    first, second = jax.random.split(key)
    raw = jax.random.randint(first, (N_CTX,), 1, GROUP + 1)
    full = jax.random.randint(second, (), 0, N_CTX)
    return jnp.where(jnp.arange(N_CTX) == full, GROUP, raw).astype(jnp.int32)


def draw_queries(key, part):
    key = jax.random.fold_in(key, 3)
    result = jax.random.normal(key, (TOKENS, HEADS * HEAD_DIM), jnp.float32)
    result = jnp.clip(result, -6.0, 6.0)
    return result.astype(jnp.bfloat16)


def draw_keys(key, part):
    key = jax.random.fold_in(key, 5)
    result = jax.random.normal(key, (TOKENS, HEADS * HEAD_DIM), jnp.float32)
    result = jnp.clip(result, -6.0, 6.0)
    return result.astype(jnp.bfloat16)


def draw_lengths(key, part):
    base = token_lengths(key)
    return base


def draw_counts(key, part):
    base = token_lengths(key)
    return ((base + RATIO - 1) // RATIO).astype(jnp.int32)


def levels(stream_key, shape, pieces, least, largest):
    level, own = 1.0, jax.random.fold_in(stream_key, 6)
    for position, parts in pieces:
        heights = jnp.exp(jax.random.uniform(jax.random.fold_in(own, position), (parts,), jnp.float32, least / len(pieces), largest / len(pieces)))
        level = level * jnp.repeat(heights, shape[position] // parts).reshape([-1 if axis == position else 1 for axis in range(len(shape))])
    return level


def gaussian(rng, dims, spread, most, cuts=(), held_as=jnp.bfloat16):
    entries = spread * jax.random.normal(rng, dims, jnp.float32)
    if cuts:
        entries = entries * levels(rng, dims, cuts, -0.22, 0.18)
    return jnp.clip(entries, -most, most).astype(held_as)


def setup_inputs(seed: int = 0) -> dict:
    arg_keys = jax.random.split(jax.random.key(seed), 11)
    queries = draw_queries(jax.random.fold_in(arg_keys[10], 71), 0)
    keys = draw_keys(jax.random.fold_in(arg_keys[10], 71), 0)
    values = gaussian(arg_keys[2], (TOKENS, HEADS * HEAD_DIM), 1.0, 6.0, ((0, 16), (1, 2)))
    dout = gaussian(arg_keys[3], (TOKENS, HEADS * HEAD_DIM), 1.0, 6.0, ((0, 16), (1, 2)))
    beacon_keys = gaussian(arg_keys[4], (BEACONS, HEADS * HEAD_DIM), 1.0, 6.0, ((0, 16), (1, 2)))
    beacon_values = gaussian(arg_keys[5], (BEACONS, HEADS * HEAD_DIM), 1.0, 6.0, ((0, 16), (1, 2)))
    beacon_key_weight = gaussian(arg_keys[6], (D, HEADS * HEAD_DIM), (HEADS * HEAD_DIM) ** -0.5, 0.125, ((0, 16), (1, 2)))
    beacon_value_weight = gaussian(arg_keys[7], (D, HEADS * HEAD_DIM), (HEADS * HEAD_DIM) ** -0.5, 0.125, ((0, 16), (1, 2)))
    lengths = draw_lengths(jax.random.fold_in(arg_keys[10], 71), 0)
    counts = draw_counts(jax.random.fold_in(arg_keys[10], 71), 0)
    return {"queries": queries, "keys": keys, "values": values, "dout": dout, "beacon_keys": beacon_keys, "beacon_values": beacon_values, "beacon_key_weight": beacon_key_weight, "beacon_value_weight": beacon_value_weight, "lengths": lengths, "counts": counts}


def group_masks(group_id, lengths, counts, rows, beacon_rows, per_group):
    group_ids = jnp.arange(lengths.shape[0], dtype=jnp.int32)
    length = jnp.sum(jnp.where(group_ids == group_id, lengths, 0))
    positions = jnp.arange(rows, dtype=jnp.int32)
    raw_mask = (positions[None, :] <= positions[:, None]) & (positions[None, :] < length)
    slots = jnp.arange(beacon_rows, dtype=jnp.int32)
    owners = slots // per_group
    owner_count = jnp.sum(jnp.where(owners[:, None] == group_ids[None, :], counts[None, :], 0), axis=1)
    beacon_mask = (owners < group_id) & (slots % per_group < owner_count)
    return raw_mask, beacon_mask, positions < length


def product(form, left, right):
    return jnp.einsum(form, left.astype(jnp.float32), right.astype(jnp.float32), precision=lax.Precision.HIGHEST)


def head_pass(qh, kh, vh, doh, bkh, bvh, raw_mask, beacon_mask, scale):
    rows = kh.shape[0]
    keys_all = jnp.concatenate([kh, bkh], axis=0)
    vals_all = jnp.concatenate([vh, bvh], axis=0)
    mask = jnp.concatenate([raw_mask, jnp.broadcast_to(beacon_mask[None, :], (qh.shape[0], bkh.shape[0]))], axis=1)
    scores = product("td,sd->ts", qh, keys_all) * scale
    scores = jnp.where(mask, scores, -jnp.inf)
    top = jnp.max(scores, axis=1, keepdims=True)
    expo = jnp.exp(scores - top)
    probs = expo / jnp.sum(expo, axis=1, keepdims=True)
    probs_low = probs.astype(jnp.bfloat16)
    output = product("ts,sd->td", probs_low, vals_all)
    delta = jnp.sum(doh.astype(jnp.float32) * output, axis=1, keepdims=True)
    dprobs = product("td,sd->ts", doh, vals_all)
    dscores = (probs * (dprobs - delta) * scale).astype(jnp.bfloat16)
    dq = product("ts,sd->td", dscores, keys_all).astype(jnp.bfloat16)
    dk = product("ts,td->sd", dscores[:, :rows], qh).astype(jnp.bfloat16)
    dv = product("ts,td->sd", probs_low[:, :rows], doh).astype(jnp.bfloat16)
    dkb = product("ts,td->sd", dscores[:, rows:], qh)
    dvb = product("ts,td->sd", probs_low[:, rows:], doh)
    return dq, dk, dv, dkb, dvb


def reference(queries, keys, values, dout, beacon_keys, beacon_values, beacon_key_weight, beacon_value_weight, lengths, counts):
    rows = GROUP
    scale = HEAD_DIM ** -0.5

    def split_heads(x):
        return x.reshape(x.shape[0], HEADS, HEAD_DIM).transpose(1, 0, 2)

    beacon_k = split_heads(beacon_keys)
    beacon_v = split_heads(beacon_values)
    beacon_rows = beacon_keys.shape[0]

    def one_group(carry, group_id):
        start = group_id * rows

        def cut(x):
            return split_heads(lax.dynamic_slice_in_dim(x, start, rows, 0))

        raw_mask, beacon_mask, valid = group_masks(group_id, lengths, counts, rows, beacon_rows, BEACON)
        grad_out = cut(dout)
        grad_out = jnp.where(valid[None, :, None], grad_out, jnp.zeros_like(grad_out))

        def per_head(qh, kh, vh, doh, bkh, bvh):
            return head_pass(qh, kh, vh, doh, bkh, bvh, raw_mask, beacon_mask, scale)

        dq, dk, dv, dkb, dvb = jax.vmap(per_head)(cut(queries), cut(keys), cut(values), grad_out, beacon_k, beacon_v)
        return (carry[0] + dkb, carry[1] + dvb), (dq, dk, dv)

    zeros = jnp.zeros((HEADS, beacon_rows, HEAD_DIM), jnp.float32)
    sums, grads = lax.scan(one_group, (zeros, zeros), jnp.arange(N_CTX, dtype=jnp.int32))

    def merge_tokens(x):
        return x.transpose(0, 2, 1, 3).reshape(N_CTX * rows, HEADS * HEAD_DIM)

    def merge_beacons(x):
        return x.transpose(1, 0, 2).reshape(beacon_rows, HEADS * HEAD_DIM).astype(jnp.bfloat16)

    beacon_key_grad = merge_beacons(sums[0])
    beacon_value_grad = merge_beacons(sums[1])
    hidden = jnp.dot(beacon_key_grad, beacon_key_weight.T, preferred_element_type=jnp.float32)
    hidden = hidden + jnp.dot(beacon_value_grad, beacon_value_weight.T, preferred_element_type=jnp.float32)
    return (merge_tokens(grads[0]), merge_tokens(grads[1]), merge_tokens(grads[2]),
            beacon_key_grad, beacon_value_grad, hidden.astype(jnp.bfloat16))
```

```python
import functools

import jax
import jax.numpy as jnp
from jax import lax
from jax.experimental import pallas as pl
from jax.experimental.pallas import tpu as pltpu
from jax.sharding import PartitionSpec as P

HEAD_DIM = 128
LOG2E = 1.4426950408889634
NEG = -1e30


def dot_nt(a, b):
    return lax.dot_general(a, b, (((1,), (1,)), ((), ())), preferred_element_type=jnp.float32)


def dot_nn(a, b):
    return lax.dot_general(a, b, (((1,), (0,)), ((), ())), preferred_element_type=jnp.float32)


def dot_tn(a, b):
    return lax.dot_general(a, b, (((0,), (0,)), ((), ())), preferred_element_type=jnp.float32)


def fill_bias(bias, lengths_ref, counts_ref, me, rows, n_groups, per_group):
    length = lengths_ref[me]
    key_slot = lax.broadcasted_iota(jnp.int32, (rows, rows), 0)
    query_slot = lax.broadcasted_iota(jnp.int32, (rows, rows), 1)
    raw = (key_slot <= query_slot) & (key_slot < length)
    bias[0:rows, :] = jnp.where(raw, 0.0, NEG)
    slot = lax.broadcasted_iota(jnp.int32, (per_group, rows), 0)

    def one(group, carry):
        count = jnp.where(group < me, counts_ref[group], 0)
        at = pl.multiple_of(rows + group * per_group, per_group)
        bias[pl.ds(at, per_group), :] = jnp.where(slot < count, 0.0, NEG)
        return carry

    lax.fori_loop(0, n_groups, one, 0)


def attention_kernel(
    n_groups, lengths_ref, counts_ref, q_ref, k_ref, v_ref, g_ref, bk_ref, bv_ref,
    dq_ref, dk_ref, dv_ref, dkb_ref, dvb_ref, bias,
):
    rows, width = q_ref.shape
    per_group = bk_ref.shape[0] // n_groups
    me = lax.axis_index("ctx")
    fill_bias(bias, lengths_ref, counts_ref, me, rows, n_groups, per_group)
    scale = HEAD_DIM**-0.5
    valid = lax.broadcasted_iota(jnp.int32, (rows, HEAD_DIM), 0) < lengths_ref[me]

    for head in range(width // HEAD_DIM):
        cols = slice(head * HEAD_DIM, (head + 1) * HEAD_DIM)
        q = q_ref[:, cols]
        g = jnp.where(valid, g_ref[:, cols], jnp.zeros((rows, HEAD_DIM), jnp.bfloat16))
        keys = jnp.concatenate([k_ref[:, cols], bk_ref[:, cols]], axis=0)
        vals = jnp.concatenate([v_ref[:, cols], bv_ref[:, cols]], axis=0)
        scores = dot_nt(keys, q) * (scale * LOG2E) + bias[...]
        top = jnp.max(scores, axis=0, keepdims=True)
        expo = jnp.exp2(scores - top)
        total = jnp.sum(expo, axis=0, keepdims=True)
        probs = expo * (1.0 / total)
        low = probs.astype(jnp.bfloat16)
        dprobs = dot_nt(vals, g)
        delta = jnp.sum(low.astype(jnp.float32) * dprobs, axis=0, keepdims=True)
        dscores = (probs * ((dprobs - delta) * scale)).astype(jnp.bfloat16)
        dq_ref[:, cols] = dot_tn(keys, dscores).T.astype(jnp.bfloat16)
        dkeys = dot_nn(dscores, q)
        dvals = dot_nn(low, g)
        dk_ref[:, cols] = dkeys[:rows].astype(jnp.bfloat16)
        dv_ref[:, cols] = dvals[:rows].astype(jnp.bfloat16)
        dkb_ref[:, cols] = dkeys[rows:].astype(jnp.bfloat16)
        dvb_ref[:, cols] = dvals[rows:].astype(jnp.bfloat16)


def attention(q, k, v, g, bk, bv, lengths, counts):
    n_groups = lengths.shape[0]
    rows, width = q.shape
    slots = bk.shape[0]
    vmem = pl.BlockSpec(memory_space=pltpu.VMEM)
    smem = pl.BlockSpec(memory_space=pltpu.SMEM)
    low = jnp.bfloat16
    raw = jax.ShapeDtypeStruct((rows, width), low)
    beacon = jax.ShapeDtypeStruct((slots, width), low)
    return pl.pallas_call(
        functools.partial(attention_kernel, n_groups),
        out_shape=(raw, raw, raw, beacon, beacon),
        in_specs=[smem, smem] + [vmem] * 6,
        out_specs=(vmem,) * 5,
        scratch_shapes=[pltpu.VMEM((rows + slots, rows), jnp.float32)],
        compiler_params=pltpu.CompilerParams(vmem_limit_bytes=48 * 1024 * 1024),
    )(lengths, counts, q, k, v, g, bk, bv)


def per_device(
    queries,
    keys,
    values,
    dout,
    beacon_keys,
    beacon_values,
    beacon_key_weight,
    beacon_value_weight,
    lengths,
    counts,
):
    width = queries.shape[1]
    both = jnp.concatenate([beacon_keys, beacon_values], axis=1)
    gathered = lax.all_gather(both, "ctx", axis=0, tiled=True)
    query_grad, key_grad, value_grad, dkb, dvb = attention(
        queries, keys, values, dout, gathered[:, :width], gathered[:, width:], lengths, counts
    )
    terms = jnp.concatenate([dkb, dvb], axis=1)
    summed = lax.psum_scatter(terms, "ctx", scatter_dimension=0, tiled=True)
    all_grads = lax.all_gather(summed, "ctx", axis=0, tiled=True)
    weights = jnp.concatenate([beacon_key_weight, beacon_value_weight], axis=1)
    part = dot_nt(all_grads, weights).astype(jnp.bfloat16)
    mine = lax.all_to_all(part, "ctx", split_axis=0, concat_axis=1, tiled=True)
    hidden = lax.psum_scatter(mine, "head", scatter_dimension=1, tiled=True)
    return (query_grad, key_grad, value_grad, summed[:, :width], summed[:, width:], hidden)


def solution(mesh):
    spec = P("ctx", "head")
    return jax.shard_map(
        per_device,
        mesh=mesh,
        in_specs=(spec,) * 8 + (P(), P()),
        out_specs=(spec,) * 6,
        check_vma=False,
    )
```

```python
import functools

import jax
import jax.numpy as jnp
from jax import lax
from jax.experimental import pallas as pl
from jax.experimental.pallas import tpu as pltpu
from jax.sharding import PartitionSpec as P

HEAD_DIM = 128
LOG2E = 1.4426950408889634
NEG = -1e30


def dot_nt(a, b):
    return lax.dot_general(a, b, (((1,), (1,)), ((), ())), preferred_element_type=jnp.float32)


def dot_nn(a, b):
    return lax.dot_general(a, b, (((1,), (0,)), ((), ())), preferred_element_type=jnp.float32)


def dot_tn(a, b):
    return lax.dot_general(a, b, (((0,), (0,)), ((), ())), preferred_element_type=jnp.float32)


def fill_bias(bias, lengths_ref, counts_ref, me, rows, n_groups, per_group):
    length = lengths_ref[me]
    key_slot = lax.broadcasted_iota(jnp.int32, (rows, rows), 0)
    query_slot = lax.broadcasted_iota(jnp.int32, (rows, rows), 1)
    raw = (key_slot <= query_slot) & (key_slot < length)
    bias[0:rows, :] = jnp.where(raw, 0.0, NEG)
    slot = lax.broadcasted_iota(jnp.int32, (per_group, rows), 0)

    def one(group, carry):
        count = jnp.where(group < me, counts_ref[group], 0)
        at = pl.multiple_of(rows + group * per_group, per_group)
        bias[pl.ds(at, per_group), :] = jnp.where(slot < count, 0.0, NEG)
        return carry

    lax.fori_loop(0, n_groups, one, 0)


def attention_kernel(
    n_groups, lengths_ref, counts_ref, q_ref, k_ref, v_ref, g_ref, beacon_ref,
    dq_ref, dk_ref, dv_ref, terms_ref, bias,
):
    rows, width = q_ref.shape
    per_group = beacon_ref.shape[0] // n_groups
    me = lax.axis_index("ctx")
    fill_bias(bias, lengths_ref, counts_ref, me, rows, n_groups, per_group)
    scale = HEAD_DIM**-0.5
    valid = lax.broadcasted_iota(jnp.int32, (rows, HEAD_DIM), 0) < lengths_ref[me]

    for head in range(width // HEAD_DIM):
        cols = slice(head * HEAD_DIM, (head + 1) * HEAD_DIM)
        q = q_ref[:, cols]
        g = jnp.where(valid, g_ref[:, cols], jnp.zeros((rows, HEAD_DIM), jnp.bfloat16))
        late = slice(width + head * HEAD_DIM, width + (head + 1) * HEAD_DIM)
        keys = jnp.concatenate([k_ref[:, cols], beacon_ref[:, cols]], axis=0)
        vals = jnp.concatenate([v_ref[:, cols], beacon_ref[:, late]], axis=0)
        scores = dot_nt(keys, q) * (scale * LOG2E) + bias[...]
        top = jnp.max(scores, axis=0, keepdims=True)
        expo = jnp.exp2(scores - top)
        total = jnp.sum(expo, axis=0, keepdims=True)
        probs = expo * (1.0 / total)
        low = probs.astype(jnp.bfloat16)
        dprobs = dot_nt(vals, g)
        delta = jnp.sum(low.astype(jnp.float32) * dprobs, axis=0, keepdims=True)
        dscores = (probs * ((dprobs - delta) * scale)).astype(jnp.bfloat16)
        dq_ref[:, cols] = dot_tn(keys, dscores).T.astype(jnp.bfloat16)
        dkeys = dot_nn(dscores, q)
        dvals = dot_nn(low, g)
        dk_ref[:, cols] = dkeys[:rows].astype(jnp.bfloat16)
        dv_ref[:, cols] = dvals[:rows].astype(jnp.bfloat16)
        terms_ref[:, cols] = dkeys[rows:].astype(jnp.bfloat16)
        terms_ref[:, late] = dvals[rows:].astype(jnp.bfloat16)


def attention(q, k, v, g, beacons, lengths, counts):
    n_groups = lengths.shape[0]
    rows, width = q.shape
    slots = beacons.shape[0]
    vmem = pl.BlockSpec(memory_space=pltpu.VMEM)
    smem = pl.BlockSpec(memory_space=pltpu.SMEM)
    raw = jax.ShapeDtypeStruct((rows, width), jnp.bfloat16)
    return pl.pallas_call(
        functools.partial(attention_kernel, n_groups),
        out_shape=(raw, raw, raw, jax.ShapeDtypeStruct(beacons.shape, jnp.bfloat16)),
        in_specs=[smem, smem] + [vmem] * 5,
        out_specs=(vmem,) * 4,
        scratch_shapes=[pltpu.VMEM((rows + slots, rows), jnp.float32)],
        compiler_params=pltpu.CompilerParams(vmem_limit_bytes=48 * 1024 * 1024),
    )(lengths, counts, q, k, v, g, beacons)


class Grid:
    def __init__(self, n):
        self.C = 2
        chips = n // 2
        self.X = 1
        while self.X * self.X * 4 <= chips:
            self.X *= 2
        self.Z = chips // self.X
        self.me = lax.axis_index("ctx")
        self.c = lax.rem(self.me, 2)
        self.x = lax.rem(self.me // 2, self.X)
        self.z = self.me // (2 * self.X)
        self.up, self.down = self.me + 2 * self.X, self.me - 2 * self.X
        self.partner = self.me + 1 - 2 * self.c

    def at(self, z, x, c):
        return (z * self.X + x) * 2 + c

    def greet(self):
        barrier = pltpu.get_barrier_semaphore()

        def hello(ctx):
            pl.semaphore_signal(
                barrier, inc=1, device_id={"ctx": ctx}, device_id_type=pl.DeviceIdType.MESH
            )

        hello(self.partner)
        for dx in range(1, self.X):
            hello(self.at(self.z, lax.rem(self.x + dx, self.X), self.c))
        pl.when(self.z < self.Z - 1)(lambda: hello(self.up))
        pl.when(self.z > 0)(lambda: hello(self.down))
        ends = jnp.where(self.z > 0, 1, 0) + jnp.where(self.z < self.Z - 1, 1, 0)
        return barrier, self.X + ends


def remote(src, dst, send, recv, ctx, head=None):
    where = {"ctx": ctx} if head is None else {"ctx": ctx, "head": head}
    return pltpu.make_async_remote_copy(
        src_ref=src, dst_ref=dst, send_sem=send, recv_sem=recv,
        device_id=where, device_id_type=pl.DeviceIdType.MESH,
    )


def spread_blocks(grid, buf, recv, z_send, x_send, c_send, both_ways):
    Z, X, z, x, c = grid.Z, grid.X, grid.z, grid.x, grid.c

    def copy(i, send, ctx):
        return remote(buf.at[i], buf.at[i], send, recv.at[i], ctx)

    def arrived(i):
        copy(i, c_send.at[i], grid.partner).wait_recv()

    def along_x(i, dx):
        return copy(i, x_send.at[i, dx - 1], grid.at(z, lax.rem(x + dx, X), c))

    def along_core(i):
        return copy(i, c_send.at[i], grid.partner)

    def along_z(i, upward):
        return copy(i, z_send.at[i, 0 if upward else 1], grid.up if upward else grid.down)

    def onward(zb, upward, downward, act):
        i = grid.at(zb, x, c)
        if upward:
            pl.when(z < Z - 1)(lambda: act(along_z(i, True)))
        if downward:
            pl.when(z > 0)(lambda: act(along_z(i, False)))
        for dx in range(1, X):
            act(along_x(i, dx))
        act(along_core(i))

    def column(s, act, wait):
        def lower():
            if wait:
                arrived(grid.at(z - s, x, c))
            onward(z - s, True, False, act)

        def upper():
            if wait:
                arrived(grid.at(z + s, x, c))
            onward(z + s, False, True, act)

        pl.when(z - s >= 0)(lower)
        if both_ways:
            pl.when(z + s < Z)(upper)

    def cross(s, act, wait):
        def row(zb):
            for dx in range(1, X):
                i = grid.at(zb, lax.rem(x + dx, X), c)
                if wait:
                    arrived(i)
                act(along_core(i))

        if s == 0:
            row(z)
            return
        pl.when(z - s >= 0)(lambda: row(z - s))
        if both_ways:
            pl.when(z + s < Z)(lambda: row(z + s))

    def start(d):
        d.start()

    def sent(d):
        d.wait_send()

    onward(z, True, both_ways, start)
    for s in range(1, Z):
        column(s, start, True)
        cross(s - 1, start, True)
    cross(Z - 1, start, True)

    def last(zb):
        for xb in range(X):
            arrived(grid.at(zb, xb, 1 - c))

    for zb in range(Z):
        if both_ways:
            last(zb)
        else:
            pl.when(zb <= z)(functools.partial(last, zb))

    def drain():
        onward(z, True, both_ways, sent)
        for s in range(1, Z):
            column(s, sent, False)
            cross(s - 1, sent, False)
        cross(Z - 1, sent, False)

    return drain


def gather_kernel(n, bk_ref, bv_ref, out_ref, recv, z_send, x_send, c_send):
    grid = Grid(n)
    width = bk_ref.shape[1]
    barrier, neighbours = grid.greet()
    out_ref[grid.me, :, 0:width] = bk_ref[...]
    out_ref[grid.me, :, width : 2 * width] = bv_ref[...]
    row = grid.X * grid.C

    for zb in range(1, grid.Z):

        def clear(zb=zb):
            part = out_ref.shape[1:]
            out_ref[zb * row : (zb + 1) * row] = jnp.zeros((row,) + part, out_ref.dtype)

        pl.when(zb > grid.z)(clear)
    pl.semaphore_wait(barrier, neighbours)
    spread_blocks(grid, out_ref, recv, z_send, x_send, c_send, False)()


def spread_sems(n):
    grid_x = 1
    while grid_x * grid_x * 4 <= n // 2:
        grid_x *= 2
    dma = pltpu.SemaphoreType.DMA
    return [dma((n,)), dma((n, 2)), dma((n, max(grid_x - 1, 1))), dma((n,))]


def gather_beacons(n, bk, bv):
    rows, width = bk.shape
    vmem = pl.BlockSpec(memory_space=pltpu.VMEM)
    return pl.pallas_call(
        functools.partial(gather_kernel, n),
        out_shape=jax.ShapeDtypeStruct((n, rows, 2 * width), jnp.bfloat16),
        in_specs=[vmem, vmem],
        out_specs=vmem,
        scratch_shapes=spread_sems(n),
        compiler_params=pltpu.CompilerParams(
            collective_id=0, has_side_effects=True, vmem_limit_bytes=48 * 1024 * 1024
        ),
    )(bk, bv)


def reduce_kernel(
    n, n_heads, terms_ref, wk_ref, wv_ref, own_ref, hidden_ref,
    grads, core_in, x_out, x_in, z_out, z_in, acc, h_out, h_in,
    recv, z_send, x_send, c_send, core_sem, xr_sem, zr_sem, h_send, h_recv,
):
    grid = Grid(n)
    Z, X, z, x, c, me = grid.Z, grid.X, grid.z, grid.x, grid.c, grid.me
    head = lax.axis_index("head")
    per_head = n // n_heads
    to_head = me // per_head
    width = wk_ref.shape[1]
    f32 = jnp.float32

    barrier, count = grid.greet()

    def hello(j, carry):
        src_c, src_h = head * per_head + j // n_heads, lax.rem(j, n_heads)

        @pl.when((src_c != me) | (src_h != head))
        def _():
            pl.semaphore_signal(
                barrier, inc=1, device_id={"ctx": src_c, "head": src_h},
                device_id_type=pl.DeviceIdType.MESH,
            )

        return carry

    lax.fori_loop(0, n, hello, 0)
    pl.semaphore_wait(barrier, count + n - jnp.where(to_head == head, 1, 0))

    def to_core(zb, xb):
        j = zb * X + xb
        return remote(
            terms_ref.at[grid.at(zb, xb, 1 - c)], core_in.at[j],
            core_sem.at[0, j], core_sem.at[1, j], grid.partner,
        )

    def to_x(zb, dx):
        return remote(
            x_out.at[zb, dx - 1], x_in.at[zb, dx - 1],
            xr_sem.at[0, zb, dx - 1], xr_sem.at[1, zb, dx - 1],
            grid.at(z, lax.rem(x + dx, X), c),
        )

    def to_z(zb):
        return remote(z_out.at[zb], z_in.at[zb], zr_sem.at[0, zb], zr_sem.at[1, zb], grid.down)

    def each_row(act):
        for zb in range(Z):
            pl.when(zb <= z)(functools.partial(act, zb))

    def core_row(zb):
        for dx in range(X):
            to_core(zb, lax.rem(x + dx, X)).start()

    each_row(core_row)

    def x_row(zb):
        for dx in list(range(1, X)) + [0]:
            xb = lax.rem(x + dx, X)
            to_core(zb, xb).wait_recv()
            total = terms_ref[grid.at(zb, xb, c)].astype(f32) + core_in[zb * X + xb].astype(f32)
            if dx == 0:
                acc[zb] = total
            else:
                x_out[zb, dx - 1] = total.astype(jnp.bfloat16)
                to_x(zb, dx).start()

    each_row(x_row)

    def z_row(zb):
        total = acc[zb]
        for dx in range(1, X):
            to_x(zb, dx).wait_recv()
            total = total + x_in[zb, dx - 1].astype(f32)
        acc[zb] = total

        @pl.when(z < Z - 1)
        def _():
            to_z(zb).wait_recv()
            acc[zb] = acc[zb] + z_in[zb].astype(f32)

        @pl.when(zb < z)
        def _():
            z_out[zb] = acc[zb].astype(jnp.bfloat16)
            to_z(zb).start()

        @pl.when(zb == z)
        def _():
            grads[me] = acc[zb].astype(jnp.bfloat16)

    each_row(z_row)
    own_ref[...] = grads[me]
    drain = spread_blocks(grid, grads, recv, z_send, x_send, c_send, True)

    rows = own_ref.shape[0]
    row = X * 2
    my_slot = (me - to_head * per_head) * n_heads + head

    def to_owner(b):
        return remote(h_out.at[b], h_in.at[my_slot], h_send.at[b], h_recv.at[my_slot], b, to_head)

    for zb in range(Z):
        block = grads[zb * row : (zb + 1) * row].reshape(row * rows, 2 * width)
        part = dot_nt(block[:, :width], wk_ref[...]) + dot_nt(block[:, width:], wv_ref[...])
        h_out[zb * row : (zb + 1) * row] = part.astype(jnp.bfloat16).reshape(row, rows, -1)

        def send(j, carry, zb=zb):
            b = zb * row + j
            here = (b == me) & (to_head == head)

            @pl.when(here)
            def _():
                h_in[my_slot] = h_out[b]

            @pl.when(jnp.logical_not(here))
            def _():
                to_owner(b).start()

            return carry

        lax.fori_loop(0, row, send, 0)

    def landed(j, carry):
        src_c, src_h = head * per_head + j // n_heads, lax.rem(j, n_heads)

        @pl.when((src_c != me) | (src_h != head))
        def _():
            remote(h_out.at[0], h_in.at[j], h_send.at[0], h_recv.at[j], me, head).wait_recv()

        return carry

    lax.fori_loop(0, n, landed, 0)
    cols = wk_ref.shape[0]
    for j in range(per_head):
        total = h_in[j * n_heads].astype(f32)
        for h in range(1, n_heads):
            total = total + h_in[j * n_heads + h].astype(f32)
        hidden_ref[:, j * cols : (j + 1) * cols] = total.astype(jnp.bfloat16)

    drain()

    def sent_row(zb):
        for dx in range(X):
            to_core(zb, lax.rem(x + dx, X)).wait_send()
        for dx in range(1, X):
            to_x(zb, dx).wait_send()
        pl.when(zb < z)(lambda: to_z(zb).wait_send())

    each_row(sent_row)

    def sent(b, carry):
        pl.when((b != me) | (to_head != head))(lambda: to_owner(b).wait_send())
        return carry

    lax.fori_loop(0, n, sent, 0)


def reduce_beacons(n, n_heads, terms, wk, wv):
    _, rows, both = terms.shape
    cols, width = wk.shape
    vmem = pl.BlockSpec(memory_space=pltpu.VMEM)
    low, dma = jnp.bfloat16, pltpu.SemaphoreType.DMA
    sems = spread_sems(n)
    X = 1
    while X * X * 4 <= n // 2:
        X *= 2
    Z, others = n // 2 // X, max(X - 1, 1)
    return pl.pallas_call(
        functools.partial(reduce_kernel, n, n_heads),
        out_shape=(
            jax.ShapeDtypeStruct((rows, both), low),
            jax.ShapeDtypeStruct((rows, cols * (n // n_heads)), low),
        ),
        in_specs=[vmem] * 3,
        out_specs=(vmem, vmem),
        scratch_shapes=[
            pltpu.VMEM((n, rows, both), low),
            pltpu.VMEM((Z * X, rows, both), low),
            pltpu.VMEM((Z, others, rows, both), low),
            pltpu.VMEM((Z, others, rows, both), low),
            pltpu.VMEM((Z, rows, both), low),
            pltpu.VMEM((Z, rows, both), low),
            pltpu.VMEM((Z, rows, both), jnp.float32),
            pltpu.VMEM((n, rows, cols), low),
            pltpu.VMEM((n, rows, cols), low),
        ]
        + sems
        + [dma((2, Z * X)), dma((2, Z, others)), dma((2, Z)), dma((n,)), dma((n,))],
        compiler_params=pltpu.CompilerParams(
            collective_id=1, has_side_effects=True, vmem_limit_bytes=48 * 1024 * 1024
        ),
    )(terms, wk, wv)


def per_device(
    n_heads,
    queries,
    keys,
    values,
    dout,
    beacon_keys,
    beacon_values,
    beacon_key_weight,
    beacon_value_weight,
    lengths,
    counts,
):
    n = lengths.shape[0]
    rows, width = beacon_keys.shape
    gathered = gather_beacons(n, beacon_keys, beacon_values)
    query_grad, key_grad, value_grad, terms = attention(
        queries, keys, values, dout, gathered.reshape(n * rows, 2 * width), lengths, counts
    )
    own, hidden = reduce_beacons(
        n, n_heads, terms.reshape(n, rows, 2 * width), beacon_key_weight, beacon_value_weight
    )
    return (query_grad, key_grad, value_grad, own[:, :width], own[:, width:], hidden)


def solution(mesh):
    spec = P("ctx", "head")
    return jax.shard_map(
        functools.partial(per_device, mesh.shape["head"]),
        mesh=mesh,
        in_specs=(spec,) * 8 + (P(), P()),
        out_specs=(spec,) * 6,
        check_vma=False,
    )
```

```python
import functools

import jax
import jax.numpy as jnp
from jax import lax
from jax.experimental import pallas as pl
from jax.experimental.pallas import tpu as pltpu
from jax.sharding import PartitionSpec as P

HEAD_DIM = 128
LOG2E = 1.4426950408889634
NEG = -1e30


def dot_nt(a, b):
    return lax.dot_general(a, b, (((1,), (1,)), ((), ())), preferred_element_type=jnp.float32)


def dot_nn(a, b):
    return lax.dot_general(a, b, (((1,), (0,)), ((), ())), preferred_element_type=jnp.float32)


def dot_tn(a, b):
    return lax.dot_general(a, b, (((0,), (0,)), ((), ())), preferred_element_type=jnp.float32)


def fill_bias(bias, lengths_ref, counts_ref, me, rows, n_groups, per_group):
    length = lengths_ref[me]
    key_slot = lax.broadcasted_iota(jnp.int32, (rows, rows), 0)
    query_slot = lax.broadcasted_iota(jnp.int32, (rows, rows), 1)
    raw = (key_slot <= query_slot) & (key_slot < length)
    bias[0:rows, :] = jnp.where(raw, 0.0, NEG)
    slot = lax.broadcasted_iota(jnp.int32, (per_group, rows), 0)

    def one(group, carry):
        count = jnp.where(group < me, counts_ref[group], 0)
        at = pl.multiple_of(rows + group * per_group, per_group)
        bias[pl.ds(at, per_group), :] = jnp.where(slot < count, 0.0, NEG)
        return carry

    lax.fori_loop(0, n_groups, one, 0)


def attend(q, k, v, g, bk, bv, bias):
    rows = q.shape[0]
    scale = HEAD_DIM**-0.5
    keys = jnp.concatenate([k, bk], axis=0)
    vals = jnp.concatenate([v, bv], axis=0)
    scores = dot_nt(keys, q) * (scale * LOG2E) + bias[...]
    top = jnp.max(scores, axis=0, keepdims=True)
    expo = jnp.exp2(scores - top)
    total = jnp.sum(expo, axis=0, keepdims=True)
    probs = expo * (1.0 / total)
    low = probs.astype(jnp.bfloat16)
    dprobs = dot_nt(vals, g)
    delta = jnp.sum(low.astype(jnp.float32) * dprobs, axis=0, keepdims=True)
    dscores = (probs * (dprobs - delta)).astype(jnp.bfloat16)
    dq = (dot_tn(keys, dscores) * scale).T.astype(jnp.bfloat16)
    dkeys = (dot_nn(dscores, q) * scale).astype(jnp.bfloat16)
    dvals = dot_nn(low, g).astype(jnp.bfloat16)
    return dq, dkeys[:rows], dvals[:rows], dkeys[rows:], dvals[rows:]


class Grid:
    def __init__(self, n):
        self.C = 2
        chips = n // 2
        self.X = 1
        while self.X * self.X * 4 <= chips:
            self.X *= 2
        self.Z = chips // self.X
        self.me = lax.axis_index("ctx")
        self.c = lax.rem(self.me, 2)
        self.x = lax.rem(self.me // 2, self.X)
        self.z = self.me // (2 * self.X)
        self.up, self.down = self.me + 2 * self.X, self.me - 2 * self.X
        self.partner = self.me + 1 - 2 * self.c

    def at(self, z, x, c):
        return (z * self.X + x) * 2 + c

    def greet(self):
        barrier = pltpu.get_barrier_semaphore()

        def hello(ctx):
            pl.semaphore_signal(
                barrier, inc=1, device_id={"ctx": ctx}, device_id_type=pl.DeviceIdType.MESH
            )

        hello(self.partner)
        for dx in range(1, self.X):
            hello(self.at(self.z, lax.rem(self.x + dx, self.X), self.c))
        pl.when(self.z < self.Z - 1)(lambda: hello(self.up))
        pl.when(self.z > 0)(lambda: hello(self.down))
        ends = jnp.where(self.z > 0, 1, 0) + jnp.where(self.z < self.Z - 1, 1, 0)
        return barrier, self.X + ends


def remote(src, dst, send, recv, ctx, head=None):
    where = {"ctx": ctx} if head is None else {"ctx": ctx, "head": head}
    return pltpu.make_async_remote_copy(
        src_ref=src, dst_ref=dst, send_sem=send, recv_sem=recv,
        device_id=where, device_id_type=pl.DeviceIdType.MESH,
    )


class Spread:
    def __init__(self, grid, buf, sems, w, both_ways, cores):
        self.grid, self.buf, self.w = grid, buf, w
        self.recv, self.z_send, self.x_send, self.c_send = sems
        self.both_ways, self.cores = both_ways, cores

    def copy(self, i, send, ctx):
        block = self.buf.at[self.w, i]
        return remote(block, block, send, self.recv.at[self.w, i], ctx)

    def arrived(self, i):
        self.along_core(i).wait_recv()

    def along_core(self, i):
        return self.copy(i, self.c_send.at[self.w, i], self.grid.partner)

    def onward(self, zb, upward, downward, act):
        grid, w = self.grid, self.w
        i = grid.at(zb, grid.x, grid.c)
        if upward:
            up = self.copy(i, self.z_send.at[w, i, 0], grid.up)
            pl.when(grid.z < grid.Z - 1)(lambda: act(up))
        if downward:
            down = self.copy(i, self.z_send.at[w, i, 1], grid.down)
            pl.when(grid.z > 0)(lambda: act(down))
        for dx in range(1, grid.X):
            there = grid.at(grid.z, lax.rem(grid.x + dx, grid.X), grid.c)
            act(self.copy(i, self.x_send.at[w, i, dx - 1], there))
        if self.cores:
            act(self.along_core(i))

    def column(self, s, act, wait):
        grid = self.grid

        def there(zb, upward):
            if wait:
                self.arrived(grid.at(zb, grid.x, grid.c))
            self.onward(zb, upward, not upward, act)

        pl.when(grid.z - s >= 0)(lambda: there(grid.z - s, True))
        if self.both_ways:
            pl.when(grid.z + s < grid.Z)(lambda: there(grid.z + s, False))

    def cross(self, s, act, wait):
        grid = self.grid

        def row(zb):
            for dx in range(1, grid.X):
                i = grid.at(zb, lax.rem(grid.x + dx, grid.X), grid.c)
                if wait:
                    self.arrived(i)
                if self.cores:
                    act(self.along_core(i))

        if s == 0:
            row(grid.z)
            return
        pl.when(grid.z - s >= 0)(lambda: row(grid.z - s))
        if self.both_ways:
            pl.when(grid.z + s < grid.Z)(lambda: row(grid.z + s))

    def own(self):
        self.onward(self.grid.z, True, self.both_ways, lambda d: d.start())

    def step(self, s):
        self.column(s, lambda d: d.start(), True)
        self.cross(s - 1, lambda d: d.start(), True)

    def finish(self):
        grid = self.grid
        self.cross(grid.Z - 1, lambda d: d.start(), True)
        if not self.cores:
            return

        def last(zb):
            for xb in range(grid.X):
                self.arrived(grid.at(zb, xb, 1 - grid.c))

        for zb in range(grid.Z):
            pl.when((zb <= grid.z) | self.both_ways)(functools.partial(last, zb))

    def drain(self):
        def sent(d):
            d.wait_send()

        self.onward(self.grid.z, True, self.both_ways, sent)
        for s in range(1, self.grid.Z):
            self.column(s, sent, False)
        if self.cores:
            for s in range(self.grid.Z):
                self.cross(s, sent, False)


class Reduce:
    def __init__(self, grid, w, terms, core_in, x_out, x_in, z_out, z_in, acc, sems):
        self.grid, self.w, self.terms, self.core_in = grid, w, terms, core_in
        self.x_out, self.x_in, self.z_out, self.z_in, self.acc = x_out, x_in, z_out, z_in, acc
        self.core_sem, self.x_sem, self.z_sem = sems

    def to_core(self, zb, xb):
        grid, w = self.grid, self.w
        j = zb * grid.X + xb
        return remote(
            self.terms.at[w, grid.at(zb, xb, 1 - grid.c)], self.core_in.at[j, w],
            self.core_sem.at[0, w, j], self.core_sem.at[1, w, j], grid.partner,
        )

    def to_x(self, zb, dx):
        grid, w, d = self.grid, self.w, dx - 1
        return remote(
            self.x_out.at[zb, d, w], self.x_in.at[zb, d, w],
            self.x_sem.at[0, w, zb, d], self.x_sem.at[1, w, zb, d],
            grid.at(grid.z, lax.rem(grid.x + dx, grid.X), grid.c),
        )

    def to_z(self, zb):
        w = self.w
        return remote(
            self.z_out.at[zb, w], self.z_in.at[zb, w],
            self.z_sem.at[0, w, zb], self.z_sem.at[1, w, zb], self.grid.down,
        )

    def each_row(self, act):
        for zb in range(self.grid.Z):
            pl.when(zb <= self.grid.z)(functools.partial(act, zb))

    def start(self):
        def core_row(zb):
            for dx in range(self.grid.X):
                self.to_core(zb, lax.rem(self.grid.x + dx, self.grid.X)).start()

        self.each_row(core_row)

    def x_row(self, zb):
        grid, w = self.grid, self.w

        def act():
            for dx in list(range(1, grid.X)) + [0]:
                xb = lax.rem(grid.x + dx, grid.X)
                self.to_core(zb, xb).wait_recv()
                mine = self.terms[w, grid.at(zb, xb, grid.c)].astype(jnp.float32)
                total = mine + self.core_in[zb * grid.X + xb, w].astype(jnp.float32)
                if dx == 0:
                    self.acc[zb, w] = total
                else:
                    self.x_out[zb, dx - 1, w] = total.astype(jnp.bfloat16)
                    self.to_x(zb, dx).start()

        pl.when(zb <= grid.z)(act)

    def z_rows(self, grads):
        grid, w, acc = self.grid, self.w, self.acc

        def z_row(zb):
            total = acc[zb, w]
            for dx in range(1, grid.X):
                self.to_x(zb, dx).wait_recv()
                total = total + self.x_in[zb, dx - 1, w].astype(jnp.float32)
            acc[zb, w] = total

            @pl.when(grid.z < grid.Z - 1)
            def _():
                self.to_z(zb).wait_recv()
                acc[zb, w] = acc[zb, w] + self.z_in[zb, w].astype(jnp.float32)

            @pl.when(zb < grid.z)
            def _():
                self.z_out[zb, w] = acc[zb, w].astype(jnp.bfloat16)
                self.to_z(zb).start()

            @pl.when(zb == grid.z)
            def _():
                grads[w, grid.me] = acc[zb, w].astype(jnp.bfloat16)

        self.each_row(z_row)

    def drain(self):
        grid = self.grid

        def sent_row(zb):
            for dx in range(grid.X):
                self.to_core(zb, lax.rem(grid.x + dx, grid.X)).wait_send()
            for dx in range(1, grid.X):
                self.to_x(zb, dx).wait_send()
            pl.when(zb < grid.z)(lambda: self.to_z(zb).wait_send())

        self.each_row(sent_row)


def whole_kernel(
    n, n_heads, waves, lengths_ref, counts_ref, q_ref, k_ref, v_ref, g_ref, bk_ref, bv_ref,
    wk_ref, wv_ref,
    dq_ref, dk_ref, dv_ref, dbk_ref, dbv_ref, hidden_ref,
    bias, beacons, terms, core_in, x_out, x_in, z_out, z_in, acc, grads, weights, part, h_out, h_in,
    a_recv, a_z, a_x, a_c, d_recv, d_z, d_x, d_c, core_sem, x_sem, z_sem, w_sem, h_send, h_recv,
):
    grid = Grid(n)
    Z, X, z, c, me = grid.Z, grid.X, grid.z, grid.c, grid.me
    head = lax.axis_index("head")
    chips, per_head = n // 2, n // 2 // n_heads
    chip = me // 2
    to_head = chip // per_head
    per_group, width = bk_ref.shape
    rows = q_ref.shape[0]
    half = width // waves
    row = X * 2

    barrier, count = grid.greet()

    def source(j):
        return (head * per_head + j // n_heads) * 2 + c, lax.rem(j, n_heads)

    def hello(j, carry):
        src_c, src_h = source(j)

        @pl.when((src_c != me) | (src_h != head))
        def _():
            pl.semaphore_signal(
                barrier, inc=1, device_id={"ctx": src_c, "head": src_h},
                device_id_type=pl.DeviceIdType.MESH,
            )

        return carry

    lax.fori_loop(0, chips, hello, 0)
    for w in range(waves):
        beacons[w, me, :, 0:half] = bk_ref[:, w * half : (w + 1) * half]
        beacons[w, me, :, half : 2 * half] = bv_ref[:, w * half : (w + 1) * half]
    for zb in range(1, Z):

        def clear(zb=zb):
            zeros = jnp.zeros((row,) + beacons.shape[2:], beacons.dtype)
            for w in range(waves):
                beacons[w, zb * row : (zb + 1) * row] = zeros

        pl.when(zb > z)(clear)
    pl.semaphore_wait(barrier, count + chips - jnp.where(to_head == head, 1, 0))

    a_sems, d_sems = (a_recv, a_z, a_x, a_c), (d_recv, d_z, d_x, d_c)
    first = [Spread(grid, beacons, a_sems, w, False, True) for w in range(waves)]
    after = [Spread(grid, grads, d_sems, w, True, False) for w in range(waves)]
    sums = [
        Reduce(grid, w, terms, core_in, x_out, x_in, z_out, z_in, acc, (core_sem, x_sem, z_sem))
        for w in range(waves)
    ]
    first[0].own()
    weights[c, 0] = wk_ref[...]
    weights[c, 1] = wv_ref[...]
    fill_bias(bias, lengths_ref, counts_ref, me, rows, n, per_group)
    valid = lax.broadcasted_iota(jnp.int32, (rows, HEAD_DIM), 0) < lengths_ref[me]
    for s in range(1, Z):
        first[0].step(s)
        if s == 1:
            for w in range(1, waves):
                first[w].own()
    first[0].finish()
    to_partner = remote(
        weights.at[c], weights.at[c], w_sem.at[0], w_sem.at[1], grid.partner
    )
    to_partner.start()

    def one_head(w, slot):
        at = w * half + slot * HEAD_DIM
        cols, left = slice(at, at + HEAD_DIM), slot * HEAD_DIM
        right = half + left
        g = jnp.where(valid, g_ref[:, cols], jnp.zeros((rows, HEAD_DIM), jnp.bfloat16))
        bk = beacons[w, :, :, left : left + HEAD_DIM].reshape(n * per_group, HEAD_DIM)
        bv = beacons[w, :, :, right : right + HEAD_DIM].reshape(n * per_group, HEAD_DIM)
        dq, dk, dv, dkb, dvb = attend(q_ref[:, cols], k_ref[:, cols], v_ref[:, cols], g, bk, bv, bias)
        dq_ref[:, cols] = dq
        dk_ref[:, cols] = dk
        dv_ref[:, cols] = dv
        terms[w, :, :, left : left + HEAD_DIM] = dkb.reshape(n, per_group, HEAD_DIM)
        terms[w, :, :, right : right + HEAD_DIM] = dvb.reshape(n, per_group, HEAD_DIM)

    per_wave = half // HEAD_DIM
    for w in range(waves):
        between = []
        for s in range(1, Z):
            if w + 1 < waves:
                between.append(functools.partial(first[w + 1].step, s))
        for zb in range(Z):
            if w > 0:
                between.append(functools.partial(sums[w - 1].x_row, zb))
        for slot in range(per_wave):
            one_head(w, slot)
            for act in between[slot * len(between) // per_wave : (slot + 1) * len(between) // per_wave]:
                act()
        sums[w].start()
        if w + 1 < waves:
            first[w + 1].finish()

    top = z == Z - 1
    for w in range(waves - 1):
        pl.when(top)(functools.partial(sums[w].z_rows, grads))
    for zb in range(Z):
        sums[-1].x_row(zb)
    for w in range(waves):
        if w < waves - 1:
            pl.when(jnp.logical_not(top))(functools.partial(sums[w].z_rows, grads))
        else:
            sums[w].z_rows(grads)
        after[w].own()
        dbk_ref[:, w * half : (w + 1) * half] = grads[w, me, :, 0:half]
        dbv_ref[:, w * half : (w + 1) * half] = grads[w, me, :, half : 2 * half]
    for s in range(1, Z):
        for w in range(waves):
            after[w].step(s)

    cols = wk_ref.shape[0]
    my_slot = (chip - to_head * per_head) * n_heads + head
    to_partner.wait()

    def to_owner(b):
        return remote(
            h_out.at[b], h_in.at[my_slot], h_send.at[b], h_recv.at[my_slot], b * 2 + c, to_head
        )

    for w in range(waves):
        after[w].finish()
        span = slice(w * half, (w + 1) * half)
        for zb in range(Z):
            got = [grads[w, (zb * X + xb) * 2 + c] for xb in range(X)]
            block = jnp.concatenate(got, axis=0)
            for core in range(2):
                here = slice(core * cols, (core + 1) * cols)
                total = dot_nt(block[:, :half], weights[core, 0, :, span])
                total = total + dot_nt(block[:, half:], weights[core, 1, :, span])
                total = total.reshape(X, per_group, cols)
                if w > 0:
                    total = total + part[zb * X : (zb + 1) * X, :, here]
                if w < waves - 1:
                    part[zb * X : (zb + 1) * X, :, here] = total
                else:
                    h_out[zb * X : (zb + 1) * X, :, here] = total.astype(jnp.bfloat16)
            if w < waves - 1:
                continue
            for xb in range(X):
                b = zb * X + xb
                stays = (b == chip) & (to_head == head)

                @pl.when(stays)
                def _(b=b):
                    h_in[my_slot] = h_out[b]

                @pl.when(jnp.logical_not(stays))
                def _(b=b):
                    to_owner(b).start()

    def landed(j, carry):
        src_c, src_h = source(j)

        @pl.when((src_c != me) | (src_h != head))
        def _():
            remote(h_out.at[0], h_in.at[j], h_send.at[0], h_recv.at[j], me, head).wait_recv()

        return carry

    lax.fori_loop(0, chips, landed, 0)
    for j in range(per_head):
        total = h_in[j * n_heads].astype(jnp.float32)
        for h in range(1, n_heads):
            total = total + h_in[j * n_heads + h].astype(jnp.float32)
        hidden_ref[:, j * 2 * cols : (j + 1) * 2 * cols] = total.astype(jnp.bfloat16)

    for w in range(waves):
        first[w].drain()
        sums[w].drain()
        after[w].drain()

    def sent(b, carry):
        pl.when((b != chip) | (to_head != head))(lambda: to_owner(b).wait_send())
        return carry

    lax.fori_loop(0, chips, sent, 0)


def per_device(
    n_heads,
    queries,
    keys,
    values,
    dout,
    beacon_keys,
    beacon_values,
    beacon_key_weight,
    beacon_value_weight,
    lengths,
    counts,
):
    n = lengths.shape[0]
    rows, width = queries.shape
    per_group = beacon_keys.shape[0]
    cols = beacon_key_weight.shape[0]
    waves = 2 if (width // HEAD_DIM) % 2 == 0 else 1
    chips = n // 2
    X = 1
    while X * X * 4 <= chips:
        X *= 2
    Z, others = chips // X, max(X - 1, 1)
    low, f32, dma = jnp.bfloat16, jnp.float32, pltpu.SemaphoreType.DMA
    block = (per_group, 2 * width // waves)
    parts = (waves,) + block
    spread = [dma((waves, n)), dma((waves, n, 2)), dma((waves, n, others)), dma((waves, n))]
    raw = jax.ShapeDtypeStruct((rows, width), low)
    beacon = jax.ShapeDtypeStruct((per_group, width), low)
    vmem = pl.BlockSpec(memory_space=pltpu.VMEM)
    smem = pl.BlockSpec(memory_space=pltpu.SMEM)
    return pl.pallas_call(
        functools.partial(whole_kernel, n, n_heads, waves),
        out_shape=(
            raw, raw, raw, beacon, beacon,
            jax.ShapeDtypeStruct((per_group, cols * (n // n_heads)), low),
        ),
        in_specs=[smem, smem] + [vmem] * 8,
        out_specs=(vmem,) * 6,
        scratch_shapes=[
            pltpu.VMEM((rows + n * per_group, rows), f32),
            pltpu.VMEM((waves, n) + block, low),
            pltpu.VMEM((waves, n) + block, low),
            pltpu.VMEM((chips,) + parts, low),
            pltpu.VMEM((Z, others) + parts, low),
            pltpu.VMEM((Z, others) + parts, low),
            pltpu.VMEM((Z,) + parts, low),
            pltpu.VMEM((Z,) + parts, low),
            pltpu.VMEM((Z,) + parts, f32),
            pltpu.VMEM((waves, n) + block, low),
            pltpu.VMEM((2, 2, cols, width), low),
            pltpu.VMEM((chips, per_group, 2 * cols), f32),
            pltpu.VMEM((chips, per_group, 2 * cols), low),
            pltpu.VMEM((chips, per_group, 2 * cols), low),
        ]
        + spread
        + spread
        + [
            dma((2, waves, chips)), dma((2, waves, Z, others)), dma((2, waves, Z)),
            dma((2,)), dma((chips,)), dma((chips,)),
        ],
        compiler_params=pltpu.CompilerParams(
            collective_id=0, has_side_effects=True, vmem_limit_bytes=56 * 1024 * 1024
        ),
    )(
        lengths, counts, queries, keys, values, dout, beacon_keys, beacon_values,
        beacon_key_weight, beacon_value_weight,
    )


def solution(mesh):
    spec = P("ctx", "head")
    return jax.shard_map(
        functools.partial(per_device, mesh.shape["head"]),
        mesh=mesh,
        in_specs=(spec,) * 8 + (P(), P()),
        out_specs=(spec,) * 6,
        check_vma=False,
    )
```

```python
import functools

import jax
import jax.numpy as jnp
from jax import lax
from jax.experimental import pallas as pl
from jax.experimental.pallas import tpu as pltpu
from jax.sharding import PartitionSpec as P

HEAD_DIM = 128
LOG2E = 1.4426950408889634
NEG = -1e30


def dot_nt(a, b):
    return lax.dot_general(a, b, (((1,), (1,)), ((), ())), preferred_element_type=jnp.float32)


def dot_nn(a, b):
    return lax.dot_general(a, b, (((1,), (0,)), ((), ())), preferred_element_type=jnp.float32)


def dot_tn(a, b):
    return lax.dot_general(a, b, (((0,), (0,)), ((), ())), preferred_element_type=jnp.float32)


def fill_bias(bias, lengths_ref, counts_ref, me, rows, n_groups, per_group):
    length = lengths_ref[me]
    key_slot = lax.broadcasted_iota(jnp.int32, (rows, rows), 0)
    query_slot = lax.broadcasted_iota(jnp.int32, (rows, rows), 1)
    raw = (key_slot <= query_slot) & (key_slot < length)
    bias[0:rows, :] = jnp.where(raw, 0.0, NEG)
    slot = lax.broadcasted_iota(jnp.int32, (per_group, rows), 0)

    def one(group, carry):
        count = jnp.where(group < me, counts_ref[group], 0)
        at = pl.multiple_of(rows + group * per_group, per_group)
        bias[pl.ds(at, per_group), :] = jnp.where(slot < count, 0.0, NEG)
        return carry

    lax.fori_loop(0, n_groups, one, 0)


def attend(q, k, v, g, bk, bv, bias):
    rows = q.shape[0]
    scale = HEAD_DIM**-0.5
    keys = jnp.concatenate([k, bk], axis=0)
    vals = jnp.concatenate([v, bv], axis=0)
    scores = dot_nt(keys, q) * (scale * LOG2E) + bias[...]
    top = jnp.max(scores, axis=0, keepdims=True)
    expo = jnp.exp2(scores - top)
    total = jnp.sum(expo, axis=0, keepdims=True)
    probs = expo * (1.0 / total)
    low = probs.astype(jnp.bfloat16)
    dprobs = dot_nt(vals, g)
    delta = jnp.sum(low.astype(jnp.float32) * dprobs, axis=0, keepdims=True)
    dscores = (probs * (dprobs - delta)).astype(jnp.bfloat16)
    dq = (dot_tn(keys, dscores) * scale).T.astype(jnp.bfloat16)
    dkeys = (dot_nn(dscores, q) * scale).astype(jnp.bfloat16)
    dvals = dot_nn(low, g).astype(jnp.bfloat16)
    return dq, dkeys[:rows], dvals[:rows], dkeys[rows:], dvals[rows:]


class Grid:
    def __init__(self, n):
        self.C = 2
        chips = n // 2
        self.X = 1
        while self.X * self.X * 4 <= chips:
            self.X *= 2
        self.Z = chips // self.X
        self.me = lax.axis_index("ctx")
        self.c = lax.rem(self.me, 2)
        self.x = lax.rem(self.me // 2, self.X)
        self.z = self.me // (2 * self.X)
        self.up, self.down = self.me + 2 * self.X, self.me - 2 * self.X
        self.partner = self.me + 1 - 2 * self.c

    def at(self, z, x, c):
        return (z * self.X + x) * 2 + c

    def greet(self, n_heads):
        barrier = pltpu.get_barrier_semaphore()

        def hello(where):
            pl.semaphore_signal(
                barrier, inc=1, device_id=where, device_id_type=pl.DeviceIdType.MESH
            )

        chips = self.X * self.Z
        hello({"ctx": self.partner})
        for k in range(1, chips):
            hello({"ctx": lax.rem(self.me + 2 * k, 2 * chips)})
        head = lax.axis_index("head")
        for k in range(1, n_heads):
            hello({"head": lax.rem(head + k, n_heads)})
        return barrier, chips + n_heads - 1


def remote(src, dst, send, recv, ctx, head=None):
    where = {"ctx": ctx} if head is None else {"ctx": ctx, "head": head}
    return pltpu.make_async_remote_copy(
        src_ref=src, dst_ref=dst, send_sem=send, recv_sem=recv,
        device_id=where, device_id_type=pl.DeviceIdType.MESH,
    )


class Spread:
    def __init__(self, grid, buf, sems, w, both_ways, cores):
        self.grid, self.buf, self.w = grid, buf, w
        self.recv, self.z_send, self.x_send, self.c_send = sems
        self.both_ways, self.cores = both_ways, cores

    def copy(self, i, send, ctx):
        block = self.buf.at[self.w, i]
        return remote(block, block, send, self.recv.at[self.w, i], ctx)

    def arrived(self, i):
        self.along_core(i).wait_recv()

    def along_core(self, i):
        return self.copy(i, self.c_send.at[self.w, i], self.grid.partner)

    def onward(self, zb, upward, downward, act):
        grid, w = self.grid, self.w
        i = grid.at(zb, grid.x, grid.c)
        if upward:
            up = self.copy(i, self.z_send.at[w, i, 0], grid.up)
            pl.when(grid.z < grid.Z - 1)(lambda: act(up))
        if downward:
            down = self.copy(i, self.z_send.at[w, i, 1], grid.down)
            pl.when(grid.z > 0)(lambda: act(down))
        for dx in range(1, grid.X):
            there = grid.at(grid.z, lax.rem(grid.x + dx, grid.X), grid.c)
            act(self.copy(i, self.x_send.at[w, i, dx - 1], there))
        if self.cores:
            act(self.along_core(i))

    def column(self, s, act, wait):
        grid = self.grid

        def there(zb, upward):
            if wait:
                self.arrived(grid.at(zb, grid.x, grid.c))
            self.onward(zb, upward, not upward, act)

        pl.when(grid.z - s >= 0)(lambda: there(grid.z - s, True))
        if self.both_ways:
            pl.when(grid.z + s < grid.Z)(lambda: there(grid.z + s, False))

    def cross(self, s, act, wait):
        grid = self.grid

        def row(zb):
            for dx in range(1, grid.X):
                i = grid.at(zb, lax.rem(grid.x + dx, grid.X), grid.c)
                if wait:
                    self.arrived(i)
                if self.cores:
                    act(self.along_core(i))

        if s == 0:
            row(grid.z)
            return
        pl.when(grid.z - s >= 0)(lambda: row(grid.z - s))
        if self.both_ways:
            pl.when(grid.z + s < grid.Z)(lambda: row(grid.z + s))

    def own(self):
        self.onward(self.grid.z, True, self.both_ways, lambda d: d.start())

    def step(self, s):
        self.column(s, lambda d: d.start(), True)
        self.cross(s - 1, lambda d: d.start(), True)

    def finish(self):
        grid = self.grid
        self.cross(grid.Z - 1, lambda d: d.start(), True)
        if not self.cores:
            return

        def last(zb):
            for xb in range(grid.X):
                self.arrived(grid.at(zb, xb, 1 - grid.c))

        for zb in range(grid.Z):
            pl.when((zb <= grid.z) | self.both_ways)(functools.partial(last, zb))

    def drain(self):
        def sent(d):
            d.wait_send()

        self.onward(self.grid.z, True, self.both_ways, sent)
        for s in range(1, self.grid.Z):
            self.column(s, sent, False)
        if self.cores:
            for s in range(self.grid.Z):
                self.cross(s, sent, False)


class Reduce:
    def __init__(self, grid, w, terms, core_in, x_out, x_in, z_out, z_in, acc, sems):
        self.grid, self.w, self.terms, self.core_in = grid, w, terms, core_in
        self.x_out, self.x_in, self.z_out, self.z_in, self.acc = x_out, x_in, z_out, z_in, acc
        self.core_sem, self.x_sem, self.z_sem = sems

    def to_core(self, zb, xb):
        grid, w = self.grid, self.w
        j = zb * grid.X + xb
        return remote(
            self.terms.at[w, grid.at(zb, xb, 1 - grid.c)], self.core_in.at[j, w],
            self.core_sem.at[0, w, j], self.core_sem.at[1, w, j], grid.partner,
        )

    def to_x(self, zb, dx):
        grid, w, d = self.grid, self.w, dx - 1
        return remote(
            self.x_out.at[zb, d, w], self.x_in.at[zb, d, w],
            self.x_sem.at[0, w, zb, d], self.x_sem.at[1, w, zb, d],
            grid.at(grid.z, lax.rem(grid.x + dx, grid.X), grid.c),
        )

    def to_z(self, zb):
        w = self.w
        return remote(
            self.z_out.at[zb, w], self.z_in.at[zb, w],
            self.z_sem.at[0, w, zb], self.z_sem.at[1, w, zb], self.grid.down,
        )

    def each_row(self, act):
        for zb in range(self.grid.Z):
            pl.when(zb <= self.grid.z)(functools.partial(act, zb))

    def start(self):
        def core_row(zb):
            for dx in range(self.grid.X):
                self.to_core(zb, lax.rem(self.grid.x + dx, self.grid.X)).start()

        self.each_row(core_row)

    def x_row(self, zb):
        grid, w = self.grid, self.w

        def act():
            for dx in list(range(1, grid.X)) + [0]:
                xb = lax.rem(grid.x + dx, grid.X)
                self.to_core(zb, xb).wait_recv()
                mine = self.terms[w, grid.at(zb, xb, grid.c)].astype(jnp.float32)
                total = mine + self.core_in[zb * grid.X + xb, w].astype(jnp.float32)
                if dx == 0:
                    self.acc[zb, w] = total
                else:
                    self.x_out[zb, dx - 1, w] = total.astype(jnp.bfloat16)
                    self.to_x(zb, dx).start()

        pl.when(zb <= grid.z)(act)

    def z_rows(self, grads):
        grid, w, acc = self.grid, self.w, self.acc

        def z_row(zb):
            total = acc[zb, w]
            for dx in range(1, grid.X):
                self.to_x(zb, dx).wait_recv()
                total = total + self.x_in[zb, dx - 1, w].astype(jnp.float32)
            acc[zb, w] = total

            @pl.when(grid.z < grid.Z - 1)
            def _():
                self.to_z(zb).wait_recv()
                acc[zb, w] = acc[zb, w] + self.z_in[zb, w].astype(jnp.float32)

            @pl.when(zb < grid.z)
            def _():
                self.z_out[zb, w] = acc[zb, w].astype(jnp.bfloat16)
                self.to_z(zb).start()

            @pl.when(zb == grid.z)
            def _():
                grads[w, grid.me] = acc[zb, w].astype(jnp.bfloat16)

        self.each_row(z_row)

    def drain(self):
        grid = self.grid

        def sent_row(zb):
            for dx in range(grid.X):
                self.to_core(zb, lax.rem(grid.x + dx, grid.X)).wait_send()
            for dx in range(1, grid.X):
                self.to_x(zb, dx).wait_send()
            pl.when(zb < grid.z)(lambda: self.to_z(zb).wait_send())

        self.each_row(sent_row)


def whole_kernel(
    n, n_heads, waves, lengths_ref, counts_ref, q_ref, k_ref, v_ref, g_ref, bk_ref, bv_ref,
    wk_ref, wv_ref,
    dq_ref, dk_ref, dv_ref, dbk_ref, dbv_ref, hidden_ref,
    bias, beacons, terms, core_in, x_out, x_in, z_out, z_in, acc, grads, weights, part, h_out, h_in, y_in,
    a_recv, a_z, a_x, a_c, d_recv, d_z, d_x, d_c, core_sem, x_sem, z_sem, w_sem, h_send, h_recv, y_send, y_recv,
):
    grid = Grid(n)
    Z, X, z, c, me = grid.Z, grid.X, grid.z, grid.c, grid.me
    head = lax.axis_index("head")
    chips, per_head = n // 2, n // 2 // n_heads
    chip = me // 2
    per_group, width = bk_ref.shape
    rows = q_ref.shape[0]
    half = width // waves
    row = X * 2

    barrier, count = grid.greet(n_heads)
    for w in range(waves):
        beacons[w, me, :, 0:half] = bk_ref[:, w * half : (w + 1) * half]
        beacons[w, me, :, half : 2 * half] = bv_ref[:, w * half : (w + 1) * half]
    for zb in range(1, Z):

        def clear(zb=zb):
            zeros = jnp.zeros((row,) + beacons.shape[2:], beacons.dtype)
            for w in range(waves):
                beacons[w, zb * row : (zb + 1) * row] = zeros

        pl.when(zb > z)(clear)
    pl.semaphore_wait(barrier, count)

    a_sems, d_sems = (a_recv, a_z, a_x, a_c), (d_recv, d_z, d_x, d_c)
    first = [Spread(grid, beacons, a_sems, w, False, True) for w in range(waves)]
    after = [Spread(grid, grads, d_sems, w, True, False) for w in range(waves)]
    sums = [
        Reduce(grid, w, terms, core_in, x_out, x_in, z_out, z_in, acc, (core_sem, x_sem, z_sem))
        for w in range(waves)
    ]
    first[0].own()
    for w in range(waves):
        span = slice(w * half, (w + 1) * half)
        weights[c, w, 0:half, :] = wk_ref[:, span].T
        weights[c, w, half : 2 * half, :] = wv_ref[:, span].T
    fill_bias(bias, lengths_ref, counts_ref, me, rows, n, per_group)
    valid = lax.broadcasted_iota(jnp.int32, (rows, HEAD_DIM), 0) < lengths_ref[me]
    for s in range(1, Z):
        first[0].step(s)
        if s == 1:
            for w in range(1, waves):
                first[w].own()
    first[0].finish()
    to_partner = remote(
        weights.at[c], weights.at[c], w_sem.at[0], w_sem.at[1], grid.partner
    )
    to_partner.start()

    def one_head(w, slot):
        at = w * half + slot * HEAD_DIM
        cols, left = slice(at, at + HEAD_DIM), slot * HEAD_DIM
        right = half + left
        g = jnp.where(valid, g_ref[:, cols], jnp.zeros((rows, HEAD_DIM), jnp.bfloat16))
        bk = beacons[w, :, :, left : left + HEAD_DIM].reshape(n * per_group, HEAD_DIM)
        bv = beacons[w, :, :, right : right + HEAD_DIM].reshape(n * per_group, HEAD_DIM)
        dq, dk, dv, dkb, dvb = attend(q_ref[:, cols], k_ref[:, cols], v_ref[:, cols], g, bk, bv, bias)
        dq_ref[:, cols] = dq
        dk_ref[:, cols] = dk
        dv_ref[:, cols] = dv
        terms[w, :, :, left : left + HEAD_DIM] = dkb.reshape(n, per_group, HEAD_DIM)
        terms[w, :, :, right : right + HEAD_DIM] = dvb.reshape(n, per_group, HEAD_DIM)

    per_wave = half // HEAD_DIM
    for w in range(waves):
        between = []
        for s in range(1, Z):
            if w + 1 < waves:
                between.append(functools.partial(first[w + 1].step, s))
        for zb in range(Z):
            if w > 0:
                between.append(functools.partial(sums[w - 1].x_row, zb))
        for slot in range(per_wave):
            one_head(w, slot)
            for act in between[slot * len(between) // per_wave : (slot + 1) * len(between) // per_wave]:
                act()
        sums[w].start()
        if w + 1 < waves:
            first[w + 1].finish()

    top = z == Z - 1
    for w in range(waves - 1):
        pl.when(top)(functools.partial(sums[w].z_rows, grads))
    for zb in range(Z):
        sums[-1].x_row(zb)
    for w in range(waves):
        if w < waves - 1:
            pl.when(jnp.logical_not(top))(functools.partial(sums[w].z_rows, grads))
        else:
            sums[w].z_rows(grads)
        after[w].own()
        dbk_ref[:, w * half : (w + 1) * half] = grads[w, me, :, 0:half]
        dbv_ref[:, w * half : (w + 1) * half] = grads[w, me, :, half : 2 * half]
    for s in range(1, Z):
        for w in range(waves):
            after[w].step(s)

    cols = wk_ref.shape[0]
    to_partner.wait()
    for w in range(waves):
        after[w].finish()
        block = jnp.concatenate([grads[w, b * 2 + c] for b in range(chips)], axis=0)
        for core in range(2):
            here = slice(core * cols, (core + 1) * cols)
            total = dot_nn(block, weights[core, w]).reshape(chips, per_group, cols)
            if w > 0:
                total = total + part[:, :, here]
            if w < waves - 1:
                part[:, :, here] = total
            else:
                h_out[:, :, here] = total.astype(jnp.bfloat16)

    def to_group(b):
        return remote(h_out.at[b], h_in.at[chip], h_send.at[b], h_recv.at[chip], b * 2 + c)

    def to_head(b, owner):
        slot = b - owner * per_head
        return remote(
            h_in.at[b], y_in.at[slot, head], y_send.at[b], y_recv.at[slot, head], me, owner
        )

    for k in range(1, chips):
        to_group(lax.rem(chip + k, chips)).start()
    h_in[chip] = h_out[chip]
    for k in range(chips):
        b = lax.rem(chip + k, chips)
        if k > 0:
            remote(h_out.at[0], h_in.at[b], h_send.at[0], h_recv.at[b], me).wait_recv()
        owner = b // per_head
        pl.when(owner != head)(lambda b=b, owner=owner: to_head(b, owner).start())
    for j in range(per_head):
        total = h_in[head * per_head + j].astype(jnp.float32)
        for k in range(1, n_heads):
            other = lax.rem(head + k, n_heads)
            remote(
                h_in.at[0], y_in.at[j, other], y_send.at[0], y_recv.at[j, other], me, other
            ).wait_recv()
            total = total + y_in[j, other].astype(jnp.float32)
        hidden_ref[:, j * 2 * cols : (j + 1) * 2 * cols] = total.astype(jnp.bfloat16)

    for w in range(waves):
        first[w].drain()
        sums[w].drain()
        after[w].drain()

    for k in range(chips):
        b = lax.rem(chip + k, chips)
        if k > 0:
            to_group(b).wait_send()
        owner = b // per_head
        pl.when(owner != head)(lambda b=b, owner=owner: to_head(b, owner).wait_send())


def per_device(
    n_heads,
    queries,
    keys,
    values,
    dout,
    beacon_keys,
    beacon_values,
    beacon_key_weight,
    beacon_value_weight,
    lengths,
    counts,
):
    n = lengths.shape[0]
    rows, width = queries.shape
    per_group = beacon_keys.shape[0]
    cols = beacon_key_weight.shape[0]
    waves = 2 if (width // HEAD_DIM) % 2 == 0 else 1
    chips = n // 2
    X = 1
    while X * X * 4 <= chips:
        X *= 2
    Z, others = chips // X, max(X - 1, 1)
    low, f32, dma = jnp.bfloat16, jnp.float32, pltpu.SemaphoreType.DMA
    block = (per_group, 2 * width // waves)
    parts = (waves,) + block
    spread = [dma((waves, n)), dma((waves, n, 2)), dma((waves, n, others)), dma((waves, n))]
    raw = jax.ShapeDtypeStruct((rows, width), low)
    beacon = jax.ShapeDtypeStruct((per_group, width), low)
    vmem = pl.BlockSpec(memory_space=pltpu.VMEM)
    smem = pl.BlockSpec(memory_space=pltpu.SMEM)
    return pl.pallas_call(
        functools.partial(whole_kernel, n, n_heads, waves),
        out_shape=(
            raw, raw, raw, beacon, beacon,
            jax.ShapeDtypeStruct((per_group, cols * (n // n_heads)), low),
        ),
        in_specs=[smem, smem] + [vmem] * 8,
        out_specs=(vmem,) * 6,
        scratch_shapes=[
            pltpu.VMEM((rows + n * per_group, rows), f32),
            pltpu.VMEM((waves, n) + block, low),
            pltpu.VMEM((waves, n) + block, low),
            pltpu.VMEM((chips,) + parts, low),
            pltpu.VMEM((Z, others) + parts, low),
            pltpu.VMEM((Z, others) + parts, low),
            pltpu.VMEM((Z,) + parts, low),
            pltpu.VMEM((Z,) + parts, low),
            pltpu.VMEM((Z,) + parts, f32),
            pltpu.VMEM((waves, n) + block, low),
            pltpu.VMEM((2, waves, 2 * width // waves, cols), low),
            pltpu.VMEM((chips, per_group, 2 * cols), f32),
            pltpu.VMEM((chips, per_group, 2 * cols), low),
            pltpu.VMEM((chips, per_group, 2 * cols), low),
            pltpu.VMEM((chips // n_heads, n_heads, per_group, 2 * cols), low),
        ]
        + spread
        + spread
        + [
            dma((2, waves, chips)), dma((2, waves, Z, others)), dma((2, waves, Z)),
            dma((2,)), dma((chips,)), dma((chips,)), dma((chips,)), dma((chips // n_heads, n_heads)),
        ],
        compiler_params=pltpu.CompilerParams(
            collective_id=0, has_side_effects=True, vmem_limit_bytes=56 * 1024 * 1024
        ),
    )(
        lengths, counts, queries, keys, values, dout, beacon_keys, beacon_values,
        beacon_key_weight, beacon_value_weight,
    )


def solution(mesh):
    spec = P("ctx", "head")
    return jax.shard_map(
        functools.partial(per_device, mesh.shape["head"]),
        mesh=mesh,
        in_specs=(spec,) * 8 + (P(), P()),
        out_specs=(spec,) * 6,
        check_vma=False,
    )
```

```python
import functools

import jax
import jax.numpy as jnp
from jax import lax
from jax.experimental import pallas as pl
from jax.experimental.pallas import tpu as pltpu
from jax.sharding import PartitionSpec as P

HEAD_DIM = 128
LOG2E = 1.4426950408889634
NEG = -1e30


def dot_nt(a, b):
    return lax.dot_general(a, b, (((1,), (1,)), ((), ())), preferred_element_type=jnp.float32)


def dot_nn(a, b):
    return lax.dot_general(a, b, (((1,), (0,)), ((), ())), preferred_element_type=jnp.float32)


def dot_tn(a, b):
    return lax.dot_general(a, b, (((0,), (0,)), ((), ())), preferred_element_type=jnp.float32)


def fill_bias(bias, lengths_ref, counts_ref, me, rows, n_groups, per_group):
    length = lengths_ref[me]
    key_slot = lax.broadcasted_iota(jnp.int32, (rows, rows), 0)
    query_slot = lax.broadcasted_iota(jnp.int32, (rows, rows), 1)
    raw = (key_slot <= query_slot) & (key_slot < length)
    bias[0:rows, :] = jnp.where(raw, 0.0, NEG)
    slot = lax.broadcasted_iota(jnp.int32, (per_group, rows), 0)

    def one(group, carry):
        count = jnp.where(group < me, counts_ref[group], 0)
        at = pl.multiple_of(rows + group * per_group, per_group)
        bias[pl.ds(at, per_group), :] = jnp.where(slot < count, 0.0, NEG)
        return carry

    lax.fori_loop(0, n_groups, one, 0)


def attention_kernel(
    n_groups, lengths_ref, counts_ref, q_ref, k_ref, v_ref, g_ref, beacon_ref,
    dq_ref, dk_ref, dv_ref, terms_ref, bias,
):
    rows, width = q_ref.shape
    per_group = beacon_ref.shape[0] // n_groups
    me = lax.axis_index("ctx")
    fill_bias(bias, lengths_ref, counts_ref, me, rows, n_groups, per_group)
    scale = HEAD_DIM**-0.5
    valid = lax.broadcasted_iota(jnp.int32, (rows, HEAD_DIM), 0) < lengths_ref[me]

    for head in range(width // HEAD_DIM):
        cols = slice(head * HEAD_DIM, (head + 1) * HEAD_DIM)
        q = q_ref[:, cols]
        g = jnp.where(valid, g_ref[:, cols], jnp.zeros((rows, HEAD_DIM), jnp.bfloat16))
        late = slice(width + head * HEAD_DIM, width + (head + 1) * HEAD_DIM)
        keys = jnp.concatenate([k_ref[:, cols], beacon_ref[:, cols]], axis=0)
        vals = jnp.concatenate([v_ref[:, cols], beacon_ref[:, late]], axis=0)
        scores = dot_nt(keys, q) * (scale * LOG2E) + bias[...]
        top = jnp.max(scores, axis=0, keepdims=True)
        expo = jnp.exp2(scores - top)
        total = jnp.sum(expo, axis=0, keepdims=True)
        probs = expo * (1.0 / total)
        low = probs.astype(jnp.bfloat16)
        dprobs = dot_nt(vals, g)
        delta = jnp.sum(low.astype(jnp.float32) * dprobs, axis=0, keepdims=True)
        dscores = (probs * ((dprobs - delta) * scale)).astype(jnp.bfloat16)
        dq_ref[:, cols] = dot_tn(keys, dscores).T.astype(jnp.bfloat16)
        dkeys = dot_nn(dscores, q)
        dvals = dot_nn(low, g)
        dk_ref[:, cols] = dkeys[:rows].astype(jnp.bfloat16)
        dv_ref[:, cols] = dvals[:rows].astype(jnp.bfloat16)
        terms_ref[:, cols] = dkeys[rows:].astype(jnp.bfloat16)
        terms_ref[:, late] = dvals[rows:].astype(jnp.bfloat16)


def attention(q, k, v, g, beacons, lengths, counts):
    n_groups = lengths.shape[0]
    rows, width = q.shape
    slots = beacons.shape[0]
    vmem = pl.BlockSpec(memory_space=pltpu.VMEM)
    smem = pl.BlockSpec(memory_space=pltpu.SMEM)
    raw = jax.ShapeDtypeStruct((rows, width), jnp.bfloat16)
    return pl.pallas_call(
        functools.partial(attention_kernel, n_groups),
        out_shape=(raw, raw, raw, jax.ShapeDtypeStruct(beacons.shape, jnp.bfloat16)),
        in_specs=[smem, smem] + [vmem] * 5,
        out_specs=(vmem,) * 4,
        scratch_shapes=[pltpu.VMEM((rows + slots, rows), jnp.float32)],
        compiler_params=pltpu.CompilerParams(vmem_limit_bytes=60 * 1024 * 1024),
    )(lengths, counts, q, k, v, g, beacons)


class Grid:
    def __init__(self, n):
        self.C = 2
        chips = n // 2
        self.X = 1
        while self.X * self.X * 4 <= chips:
            self.X *= 2
        self.Z = chips // self.X
        self.me = lax.axis_index("ctx")
        self.c = lax.rem(self.me, 2)
        self.x = lax.rem(self.me // 2, self.X)
        self.z = self.me // (2 * self.X)
        self.up, self.down = self.me + 2 * self.X, self.me - 2 * self.X
        self.partner = self.me + 1 - 2 * self.c

    def at(self, z, x, c):
        return (z * self.X + x) * 2 + c

    def greet(self):
        barrier = pltpu.get_barrier_semaphore()

        def hello(ctx):
            pl.semaphore_signal(
                barrier, inc=1, device_id={"ctx": ctx}, device_id_type=pl.DeviceIdType.MESH
            )

        hello(self.partner)
        for dx in range(1, self.X):
            hello(self.at(self.z, lax.rem(self.x + dx, self.X), self.c))
        pl.when(self.z < self.Z - 1)(lambda: hello(self.up))
        pl.when(self.z > 0)(lambda: hello(self.down))
        ends = jnp.where(self.z > 0, 1, 0) + jnp.where(self.z < self.Z - 1, 1, 0)
        return barrier, self.X + ends


def remote(src, dst, send, recv, ctx, head=None):
    where = {"ctx": ctx} if head is None else {"ctx": ctx, "head": head}
    return pltpu.make_async_remote_copy(
        src_ref=src, dst_ref=dst, send_sem=send, recv_sem=recv,
        device_id=where, device_id_type=pl.DeviceIdType.MESH,
    )


def spread_blocks(grid, buf, recv, z_send, x_send, c_send, both_ways):
    Z, X, z, x, c = grid.Z, grid.X, grid.z, grid.x, grid.c

    def copy(i, send, ctx):
        return remote(buf.at[i], buf.at[i], send, recv.at[i], ctx)

    def arrived(i):
        copy(i, c_send.at[i], grid.partner).wait_recv()

    def along_x(i, dx):
        return copy(i, x_send.at[i, dx - 1], grid.at(z, lax.rem(x + dx, X), c))

    def along_core(i):
        return copy(i, c_send.at[i], grid.partner)

    def along_z(i, upward):
        return copy(i, z_send.at[i, 0 if upward else 1], grid.up if upward else grid.down)

    def onward(zb, upward, downward, act):
        i = grid.at(zb, x, c)
        if upward:
            pl.when(z < Z - 1)(lambda: act(along_z(i, True)))
        if downward:
            pl.when(z > 0)(lambda: act(along_z(i, False)))
        for dx in range(1, X):
            act(along_x(i, dx))
        act(along_core(i))

    def column(s, act, wait):
        def lower():
            if wait:
                arrived(grid.at(z - s, x, c))
            onward(z - s, True, False, act)

        def upper():
            if wait:
                arrived(grid.at(z + s, x, c))
            onward(z + s, False, True, act)

        pl.when(z - s >= 0)(lower)
        if both_ways:
            pl.when(z + s < Z)(upper)

    def cross(s, act, wait):
        def row(zb):
            for dx in range(1, X):
                i = grid.at(zb, lax.rem(x + dx, X), c)
                if wait:
                    arrived(i)
                act(along_core(i))

        if s == 0:
            row(z)
            return
        pl.when(z - s >= 0)(lambda: row(z - s))
        if both_ways:
            pl.when(z + s < Z)(lambda: row(z + s))

    def start(d):
        d.start()

    def sent(d):
        d.wait_send()

    onward(z, True, both_ways, start)
    for s in range(1, Z):
        column(s, start, True)
        cross(s - 1, start, True)
    cross(Z - 1, start, True)

    def last(zb):
        for xb in range(X):
            arrived(grid.at(zb, xb, 1 - c))

    for zb in range(Z):
        if both_ways:
            last(zb)
        else:
            pl.when(zb <= z)(functools.partial(last, zb))

    def drain():
        onward(z, True, both_ways, sent)
        for s in range(1, Z):
            column(s, sent, False)
            cross(s - 1, sent, False)
        cross(Z - 1, sent, False)

    return drain


def gather_kernel(n, bk_ref, bv_ref, out_ref, recv, z_send, x_send, c_send):
    grid = Grid(n)
    width = bk_ref.shape[1]
    barrier, neighbours = grid.greet()
    out_ref[grid.me, :, 0:width] = bk_ref[...]
    out_ref[grid.me, :, width : 2 * width] = bv_ref[...]
    row = grid.X * grid.C

    for zb in range(1, grid.Z):

        def clear(zb=zb):
            part = out_ref.shape[1:]
            out_ref[zb * row : (zb + 1) * row] = jnp.zeros((row,) + part, out_ref.dtype)

        pl.when(zb > grid.z)(clear)
    pl.semaphore_wait(barrier, neighbours)
    spread_blocks(grid, out_ref, recv, z_send, x_send, c_send, False)()


def spread_sems(n):
    grid_x = 1
    while grid_x * grid_x * 4 <= n // 2:
        grid_x *= 2
    dma = pltpu.SemaphoreType.DMA
    return [dma((n,)), dma((n, 2)), dma((n, max(grid_x - 1, 1))), dma((n,))]


def gather_beacons(n, bk, bv):
    rows, width = bk.shape
    vmem = pl.BlockSpec(memory_space=pltpu.VMEM)
    return pl.pallas_call(
        functools.partial(gather_kernel, n),
        out_shape=jax.ShapeDtypeStruct((n, rows, 2 * width), jnp.bfloat16),
        in_specs=[vmem, vmem],
        out_specs=vmem,
        scratch_shapes=spread_sems(n),
        compiler_params=pltpu.CompilerParams(
            collective_id=0, has_side_effects=True, vmem_limit_bytes=60 * 1024 * 1024
        ),
    )(bk, bv)


def reduce_kernel(
    n, n_heads, terms_ref, wk_hbm, wv_hbm, own_ref, hidden_ref,
    wk_ref, wv_ref, w_sem,
    grads, core_in, x_out, x_in, z_out, z_in, acc, h_out, h_in,
    recv, z_send, x_send, c_send, core_sem, xr_sem, zr_sem, h_send, h_recv,
):
    grid = Grid(n)
    Z, X, z, x, c, me = grid.Z, grid.X, grid.z, grid.x, grid.c, grid.me
    head = lax.axis_index("head")
    per_head = n // n_heads
    to_head = me // per_head
    width = wk_ref.shape[1]
    f32 = jnp.float32

    own_rows = [
        pltpu.make_async_copy(wk_hbm, wk_ref, w_sem.at[0]),
        pltpu.make_async_copy(wv_hbm, wv_ref, w_sem.at[1]),
    ]
    for piece in own_rows:
        piece.start()

    barrier, count = grid.greet()

    def hello(j, carry):
        src_c, src_h = head * per_head + j // n_heads, lax.rem(j, n_heads)

        @pl.when((src_c != me) | (src_h != head))
        def _():
            pl.semaphore_signal(
                barrier, inc=1, device_id={"ctx": src_c, "head": src_h},
                device_id_type=pl.DeviceIdType.MESH,
            )

        return carry

    lax.fori_loop(0, n, hello, 0)
    pl.semaphore_wait(barrier, count + n - jnp.where(to_head == head, 1, 0))

    def to_core(zb, xb):
        j = zb * X + xb
        return remote(
            terms_ref.at[grid.at(zb, xb, 1 - c)], core_in.at[j],
            core_sem.at[0, j], core_sem.at[1, j], grid.partner,
        )

    def to_x(zb, dx):
        return remote(
            x_out.at[zb, dx - 1], x_in.at[zb, dx - 1],
            xr_sem.at[0, zb, dx - 1], xr_sem.at[1, zb, dx - 1],
            grid.at(z, lax.rem(x + dx, X), c),
        )

    def to_z(zb):
        return remote(z_out.at[zb], z_in.at[zb], zr_sem.at[0, zb], zr_sem.at[1, zb], grid.down)

    def each_row(act):
        for zb in range(Z):
            pl.when(zb <= z)(functools.partial(act, zb))

    def core_row(zb):
        for dx in range(X):
            to_core(zb, lax.rem(x + dx, X)).start()

    each_row(core_row)

    def x_row(zb):
        for dx in list(range(1, X)) + [0]:
            xb = lax.rem(x + dx, X)
            to_core(zb, xb).wait_recv()
            total = terms_ref[grid.at(zb, xb, c)].astype(f32) + core_in[zb * X + xb].astype(f32)
            if dx == 0:
                acc[zb] = total
            else:
                x_out[zb, dx - 1] = total.astype(jnp.bfloat16)
                to_x(zb, dx).start()

    def z_row(zb):
        total = acc[zb]
        for dx in range(1, X):
            to_x(zb, dx).wait_recv()
            total = total + x_in[zb, dx - 1].astype(f32)
        acc[zb] = total

        @pl.when(z < Z - 1)
        def _():
            to_z(zb).wait_recv()
            acc[zb] = acc[zb] + z_in[zb].astype(f32)

        @pl.when(zb < z)
        def _():
            z_out[zb] = acc[zb].astype(jnp.bfloat16)
            to_z(zb).start()

        @pl.when(zb == z)
        def _():
            grads[me] = acc[zb].astype(jnp.bfloat16)

    def row_or_not(act, zb):
        pl.when(zb <= z)(functools.partial(act, zb))

    row_or_not(x_row, 0)
    for zb in range(Z):
        if zb + 1 < Z:
            row_or_not(x_row, zb + 1)
        row_or_not(z_row, zb)
    own_ref[...] = grads[me]
    drain = spread_blocks(grid, grads, recv, z_send, x_send, c_send, True)

    rows = own_ref.shape[0]
    my_slot = (me - to_head * per_head) * n_heads + head

    def to_owner(b):
        return remote(h_out.at[b], h_in.at[my_slot], h_send.at[b], h_recv.at[my_slot], b, to_head)

    for piece in own_rows:
        piece.wait()
    block = grads[...].reshape(n * rows, 2 * width)
    part = dot_nt(block[:, :width], wk_ref[...]) + dot_nt(block[:, width:], wv_ref[...])
    h_out[...] = part.astype(jnp.bfloat16).reshape(n, rows, -1)

    def send(j, carry):
        b = lax.rem(me + 1 + j, n)
        here = (b == me) & (to_head == head)

        @pl.when(here)
        def _():
            h_in[my_slot] = h_out[b]

        @pl.when(jnp.logical_not(here))
        def _():
            to_owner(b).start()

        return carry

    lax.fori_loop(0, n, send, 0)

    def landed(j, carry):
        src_c, src_h = head * per_head + j // n_heads, lax.rem(j, n_heads)

        @pl.when((src_c != me) | (src_h != head))
        def _():
            remote(h_out.at[0], h_in.at[j], h_send.at[0], h_recv.at[j], me, head).wait_recv()

        return carry

    lax.fori_loop(0, n, landed, 0)
    cols = wk_ref.shape[0]
    for j in range(per_head):
        total = h_in[j * n_heads].astype(f32)
        for h in range(1, n_heads):
            total = total + h_in[j * n_heads + h].astype(f32)
        hidden_ref[:, j * cols : (j + 1) * cols] = total.astype(jnp.bfloat16)

    drain()

    def sent_row(zb):
        for dx in range(X):
            to_core(zb, lax.rem(x + dx, X)).wait_send()
        for dx in range(1, X):
            to_x(zb, dx).wait_send()
        pl.when(zb < z)(lambda: to_z(zb).wait_send())

    each_row(sent_row)

    def sent(b, carry):
        pl.when((b != me) | (to_head != head))(lambda: to_owner(b).wait_send())
        return carry

    lax.fori_loop(0, n, sent, 0)


def reduce_beacons(n, n_heads, terms, wk, wv):
    _, rows, both = terms.shape
    cols, width = wk.shape
    vmem = pl.BlockSpec(memory_space=pltpu.VMEM)
    low, dma = jnp.bfloat16, pltpu.SemaphoreType.DMA
    sems = spread_sems(n)
    X = 1
    while X * X * 4 <= n // 2:
        X *= 2
    Z, others = n // 2 // X, max(X - 1, 1)
    return pl.pallas_call(
        functools.partial(reduce_kernel, n, n_heads),
        out_shape=(
            jax.ShapeDtypeStruct((rows, both), low),
            jax.ShapeDtypeStruct((rows, cols * (n // n_heads)), low),
        ),
        in_specs=[vmem, pl.BlockSpec(memory_space=pl.ANY), pl.BlockSpec(memory_space=pl.ANY)],
        out_specs=(vmem, vmem),
        scratch_shapes=[
            pltpu.VMEM((cols, width), low),
            pltpu.VMEM((cols, width), low),
            dma((2,)),
            pltpu.VMEM((n, rows, both), low),
            pltpu.VMEM((Z * X, rows, both), low),
            pltpu.VMEM((Z, others, rows, both), low),
            pltpu.VMEM((Z, others, rows, both), low),
            pltpu.VMEM((Z, rows, both), low),
            pltpu.VMEM((Z, rows, both), low),
            pltpu.VMEM((Z, rows, both), jnp.float32),
            pltpu.VMEM((n, rows, cols), low),
            pltpu.VMEM((n, rows, cols), low),
        ]
        + sems
        + [dma((2, Z * X)), dma((2, Z, others)), dma((2, Z)), dma((n,)), dma((n,))],
        compiler_params=pltpu.CompilerParams(
            collective_id=1, has_side_effects=True, vmem_limit_bytes=60 * 1024 * 1024
        ),
    )(terms, wk, wv)


def per_device(
    n_heads,
    queries,
    keys,
    values,
    dout,
    beacon_keys,
    beacon_values,
    beacon_key_weight,
    beacon_value_weight,
    lengths,
    counts,
):
    n = lengths.shape[0]
    rows, width = beacon_keys.shape
    gathered = gather_beacons(n, beacon_keys, beacon_values)
    query_grad, key_grad, value_grad, terms = attention(
        queries, keys, values, dout, gathered.reshape(n * rows, 2 * width), lengths, counts
    )
    own, hidden = reduce_beacons(
        n, n_heads, terms.reshape(n, rows, 2 * width), beacon_key_weight, beacon_value_weight
    )
    return (query_grad, key_grad, value_grad, own[:, :width], own[:, width:], hidden)


def solution(mesh):
    spec = P("ctx", "head")
    return jax.shard_map(
        functools.partial(per_device, mesh.shape["head"]),
        mesh=mesh,
        in_specs=(spec,) * 8 + (P(), P()),
        out_specs=(spec,) * 6,
        check_vma=False,
    )
```

```python
import functools

import jax
import jax.numpy as jnp
from jax import lax
from jax.experimental import pallas as pl
from jax.experimental.pallas import tpu as pltpu
from jax.sharding import PartitionSpec as P

HEAD_DIM = 128
LOG2E = 1.4426950408889634
NEG = -1e30


def dot_nt(a, b):
    return lax.dot_general(a, b, (((1,), (1,)), ((), ())), preferred_element_type=jnp.float32)


def dot_nn(a, b):
    return lax.dot_general(a, b, (((1,), (0,)), ((), ())), preferred_element_type=jnp.float32)


def dot_tn(a, b):
    return lax.dot_general(a, b, (((0,), (0,)), ((), ())), preferred_element_type=jnp.float32)


def fill_bias(bias, lengths_ref, counts_ref, me, rows, n_groups, per_group):
    length = lengths_ref[me]
    key_slot = lax.broadcasted_iota(jnp.int32, (rows, rows), 0)
    query_slot = lax.broadcasted_iota(jnp.int32, (rows, rows), 1)
    raw = (key_slot <= query_slot) & (key_slot < length)
    bias[0:rows, :] = jnp.where(raw, 0.0, NEG)
    slot = lax.broadcasted_iota(jnp.int32, (per_group, rows), 0)

    def one(group, carry):
        count = jnp.where(group < me, counts_ref[group], 0)
        at = pl.multiple_of(rows + group * per_group, per_group)
        bias[pl.ds(at, per_group), :] = jnp.where(slot < count, 0.0, NEG)
        return carry

    lax.fori_loop(0, n_groups, one, 0)


def attention_kernel(
    n_groups, lengths_ref, counts_ref, q_ref, k_ref, v_ref, g_ref, beacon_ref,
    dq_ref, dk_ref, dv_ref, terms_ref, bias,
):
    rows, width = q_ref.shape
    per_group = beacon_ref.shape[0] // n_groups
    me = lax.axis_index("ctx")
    fill_bias(bias, lengths_ref, counts_ref, me, rows, n_groups, per_group)
    scale = HEAD_DIM**-0.5
    valid = lax.broadcasted_iota(jnp.int32, (rows, HEAD_DIM), 0) < lengths_ref[me]

    for head in range(width // HEAD_DIM):
        cols = slice(head * HEAD_DIM, (head + 1) * HEAD_DIM)
        q = q_ref[:, cols]
        g = jnp.where(valid, g_ref[:, cols], jnp.zeros((rows, HEAD_DIM), jnp.bfloat16))
        late = slice(width + head * HEAD_DIM, width + (head + 1) * HEAD_DIM)
        keys = jnp.concatenate([k_ref[:, cols], beacon_ref[:, cols]], axis=0)
        vals = jnp.concatenate([v_ref[:, cols], beacon_ref[:, late]], axis=0)
        scores = dot_nt(keys, q) * (scale * LOG2E) + bias[...]
        top = jnp.max(scores, axis=0, keepdims=True)
        expo = jnp.exp2(scores - top)
        total = jnp.sum(expo, axis=0, keepdims=True)
        probs = expo * (1.0 / total)
        low = probs.astype(jnp.bfloat16)
        dprobs = dot_nt(vals, g)
        delta = jnp.sum(low.astype(jnp.float32) * dprobs, axis=0, keepdims=True)
        dscores = (probs * ((dprobs - delta) * scale)).astype(jnp.bfloat16)
        dq_ref[:, cols] = dot_tn(keys, dscores).T.astype(jnp.bfloat16)
        dkeys = dot_nn(dscores, q)
        dvals = dot_nn(low, g)
        dk_ref[:, cols] = dkeys[:rows].astype(jnp.bfloat16)
        dv_ref[:, cols] = dvals[:rows].astype(jnp.bfloat16)
        terms_ref[:, cols] = dkeys[rows:].astype(jnp.bfloat16)
        terms_ref[:, late] = dvals[rows:].astype(jnp.bfloat16)


def attention(q, k, v, g, beacons, lengths, counts):
    n_groups = lengths.shape[0]
    rows, width = q.shape
    slots = beacons.shape[0]
    vmem = pl.BlockSpec(memory_space=pltpu.VMEM)
    smem = pl.BlockSpec(memory_space=pltpu.SMEM)
    raw = jax.ShapeDtypeStruct((rows, width), jnp.bfloat16)
    return pl.pallas_call(
        functools.partial(attention_kernel, n_groups),
        out_shape=(raw, raw, raw, jax.ShapeDtypeStruct(beacons.shape, jnp.bfloat16)),
        in_specs=[smem, smem] + [vmem] * 5,
        out_specs=(vmem,) * 4,
        scratch_shapes=[pltpu.VMEM((rows + slots, rows), jnp.float32)],
        compiler_params=pltpu.CompilerParams(vmem_limit_bytes=40 * 1024 * 1024),
    )(lengths, counts, q, k, v, g, beacons)


class Grid:
    def __init__(self, n):
        self.C = 2
        chips = n // 2
        self.X = 1
        while self.X * self.X * 4 <= chips:
            self.X *= 2
        self.Z = chips // self.X
        self.me = lax.axis_index("ctx")
        self.c = lax.rem(self.me, 2)
        self.x = lax.rem(self.me // 2, self.X)
        self.z = self.me // (2 * self.X)
        self.up, self.down = self.me + 2 * self.X, self.me - 2 * self.X
        self.partner = self.me + 1 - 2 * self.c

    def at(self, z, x, c):
        return (z * self.X + x) * 2 + c

    def greet(self):
        barrier = pltpu.get_barrier_semaphore()

        def hello(ctx):
            pl.semaphore_signal(
                barrier, inc=1, device_id={"ctx": ctx}, device_id_type=pl.DeviceIdType.MESH
            )

        hello(self.partner)
        for dx in range(1, self.X):
            hello(self.at(self.z, lax.rem(self.x + dx, self.X), self.c))
        pl.when(self.z < self.Z - 1)(lambda: hello(self.up))
        pl.when(self.z > 0)(lambda: hello(self.down))
        ends = jnp.where(self.z > 0, 1, 0) + jnp.where(self.z < self.Z - 1, 1, 0)
        return barrier, self.X + ends


def remote(src, dst, send, recv, ctx, head=None):
    where = {"ctx": ctx} if head is None else {"ctx": ctx, "head": head}
    return pltpu.make_async_remote_copy(
        src_ref=src, dst_ref=dst, send_sem=send, recv_sem=recv,
        device_id=where, device_id_type=pl.DeviceIdType.MESH,
    )


def spread_blocks(grid, buf, recv, z_send, x_send, c_send, both_ways):
    Z, X, z, x, c = grid.Z, grid.X, grid.z, grid.x, grid.c

    def copy(i, send, ctx):
        return remote(buf.at[i], buf.at[i], send, recv.at[i], ctx)

    def arrived(i):
        copy(i, c_send.at[i], grid.partner).wait_recv()

    def along_x(i, dx):
        return copy(i, x_send.at[i, dx - 1], grid.at(z, lax.rem(x + dx, X), c))

    def along_core(i):
        return copy(i, c_send.at[i], grid.partner)

    def along_z(i, upward):
        return copy(i, z_send.at[i, 0 if upward else 1], grid.up if upward else grid.down)

    def onward(zb, upward, downward, act):
        i = grid.at(zb, x, c)
        if upward:
            pl.when(z < Z - 1)(lambda: act(along_z(i, True)))
        if downward:
            pl.when(z > 0)(lambda: act(along_z(i, False)))
        for dx in range(1, X):
            act(along_x(i, dx))
        act(along_core(i))

    def column(s, act, wait):
        def lower():
            if wait:
                arrived(grid.at(z - s, x, c))
            onward(z - s, True, False, act)

        def upper():
            if wait:
                arrived(grid.at(z + s, x, c))
            onward(z + s, False, True, act)

        pl.when(z - s >= 0)(lower)
        if both_ways:
            pl.when(z + s < Z)(upper)

    def cross(s, act, wait):
        def row(zb):
            for dx in range(1, X):
                i = grid.at(zb, lax.rem(x + dx, X), c)
                if wait:
                    arrived(i)
                act(along_core(i))

        if s == 0:
            row(z)
            return
        pl.when(z - s >= 0)(lambda: row(z - s))
        if both_ways:
            pl.when(z + s < Z)(lambda: row(z + s))

    def start(d):
        d.start()

    def sent(d):
        d.wait_send()

    onward(z, True, both_ways, start)
    for s in range(1, Z):
        column(s, start, True)
        cross(s - 1, start, True)
    cross(Z - 1, start, True)

    def last(zb):
        for xb in range(X):
            arrived(grid.at(zb, xb, 1 - c))

    for zb in range(Z):
        if both_ways:
            last(zb)
        else:
            pl.when(zb <= z)(functools.partial(last, zb))

    def drain():
        onward(z, True, both_ways, sent)
        for s in range(1, Z):
            column(s, sent, False)
            cross(s - 1, sent, False)
        cross(Z - 1, sent, False)

    return drain


def gather_kernel(n, bk_ref, bv_ref, out_ref, recv, z_send, x_send, c_send):
    grid = Grid(n)
    width = bk_ref.shape[1]
    barrier, neighbours = grid.greet()
    out_ref[grid.me, :, 0:width] = bk_ref[...]
    out_ref[grid.me, :, width : 2 * width] = bv_ref[...]
    row = grid.X * grid.C

    for zb in range(1, grid.Z):

        def clear(zb=zb):
            part = out_ref.shape[1:]
            out_ref[zb * row : (zb + 1) * row] = jnp.zeros((row,) + part, out_ref.dtype)

        pl.when(zb > grid.z)(clear)
    pl.semaphore_wait(barrier, neighbours)
    spread_blocks(grid, out_ref, recv, z_send, x_send, c_send, False)()


def spread_sems(n):
    grid_x = 1
    while grid_x * grid_x * 4 <= n // 2:
        grid_x *= 2
    dma = pltpu.SemaphoreType.DMA
    return [dma((n,)), dma((n, 2)), dma((n, max(grid_x - 1, 1))), dma((n,))]


def gather_beacons(n, bk, bv):
    rows, width = bk.shape
    vmem = pl.BlockSpec(memory_space=pltpu.VMEM)
    return pl.pallas_call(
        functools.partial(gather_kernel, n),
        out_shape=jax.ShapeDtypeStruct((n, rows, 2 * width), jnp.bfloat16),
        in_specs=[vmem, vmem],
        out_specs=vmem,
        scratch_shapes=spread_sems(n),
        compiler_params=pltpu.CompilerParams(
            collective_id=0, has_side_effects=True, vmem_limit_bytes=16 * 1024 * 1024
        ),
    )(bk, bv)


def reduce_kernel(
    n, n_heads, terms_ref, wk_ref, wv_ref, own_ref, hidden_ref,
    grads, core_in, x_out, x_in, z_out, z_in, acc, h_out, h_in,
    recv, z_send, x_send, c_send, core_sem, xr_sem, zr_sem, h_send, h_recv,
):
    grid = Grid(n)
    Z, X, z, x, c, me = grid.Z, grid.X, grid.z, grid.x, grid.c, grid.me
    head = lax.axis_index("head")
    per_head = n // n_heads
    to_head = me // per_head
    width = wk_ref.shape[1]
    f32 = jnp.float32

    barrier, count = grid.greet()

    def hello(j, carry):
        src_c, src_h = head * per_head + j // n_heads, lax.rem(j, n_heads)

        @pl.when((src_c != me) | (src_h != head))
        def _():
            pl.semaphore_signal(
                barrier, inc=1, device_id={"ctx": src_c, "head": src_h},
                device_id_type=pl.DeviceIdType.MESH,
            )

        return carry

    lax.fori_loop(0, n, hello, 0)
    pl.semaphore_wait(barrier, count + n - jnp.where(to_head == head, 1, 0))

    def to_core(zb, xb):
        j = zb * X + xb
        return remote(
            terms_ref.at[grid.at(zb, xb, 1 - c)], core_in.at[j],
            core_sem.at[0, j], core_sem.at[1, j], grid.partner,
        )

    def to_x(zb, dx):
        return remote(
            x_out.at[zb, dx - 1], x_in.at[zb, dx - 1],
            xr_sem.at[0, zb, dx - 1], xr_sem.at[1, zb, dx - 1],
            grid.at(z, lax.rem(x + dx, X), c),
        )

    def to_z(zb):
        return remote(z_out.at[zb], z_in.at[zb], zr_sem.at[0, zb], zr_sem.at[1, zb], grid.down)

    def each_row(act):
        for zb in range(Z):
            pl.when(zb <= z)(functools.partial(act, zb))

    def core_row(zb):
        for dx in range(X):
            to_core(zb, lax.rem(x + dx, X)).start()

    each_row(core_row)

    def x_row(zb):
        for dx in list(range(1, X)) + [0]:
            xb = lax.rem(x + dx, X)
            to_core(zb, xb).wait_recv()
            total = terms_ref[grid.at(zb, xb, c)].astype(f32) + core_in[zb * X + xb].astype(f32)
            if dx == 0:
                acc[zb] = total
            else:
                x_out[zb, dx - 1] = total.astype(jnp.bfloat16)
                to_x(zb, dx).start()

    each_row(x_row)

    def z_row(zb):
        total = acc[zb]
        for dx in range(1, X):
            to_x(zb, dx).wait_recv()
            total = total + x_in[zb, dx - 1].astype(f32)
        acc[zb] = total

        @pl.when(z < Z - 1)
        def _():
            to_z(zb).wait_recv()
            acc[zb] = acc[zb] + z_in[zb].astype(f32)

        @pl.when(zb < z)
        def _():
            z_out[zb] = acc[zb].astype(jnp.bfloat16)
            to_z(zb).start()

        @pl.when(zb == z)
        def _():
            grads[me] = acc[zb].astype(jnp.bfloat16)

    each_row(z_row)
    own_ref[...] = grads[me]
    drain = spread_blocks(grid, grads, recv, z_send, x_send, c_send, True)

    rows = own_ref.shape[0]
    row = X * 2
    my_slot = (me - to_head * per_head) * n_heads + head

    def to_owner(b):
        return remote(h_out.at[b], h_in.at[my_slot], h_send.at[b], h_recv.at[my_slot], b, to_head)

    for zb in range(Z):
        block = grads[zb * row : (zb + 1) * row].reshape(row * rows, 2 * width)
        part = dot_nt(block[:, :width], wk_ref[...]) + dot_nt(block[:, width:], wv_ref[...])
        h_out[zb * row : (zb + 1) * row] = part.astype(jnp.bfloat16).reshape(row, rows, -1)

        def send(j, carry, zb=zb):
            b = zb * row + j
            here = (b == me) & (to_head == head)

            @pl.when(here)
            def _():
                h_in[my_slot] = h_out[b]

            @pl.when(jnp.logical_not(here))
            def _():
                to_owner(b).start()

            return carry

        lax.fori_loop(0, row, send, 0)

    def landed(j, carry):
        src_c, src_h = head * per_head + j // n_heads, lax.rem(j, n_heads)

        @pl.when((src_c != me) | (src_h != head))
        def _():
            remote(h_out.at[0], h_in.at[j], h_send.at[0], h_recv.at[j], me, head).wait_recv()

        return carry

    lax.fori_loop(0, n, landed, 0)
    cols = wk_ref.shape[0]
    for j in range(per_head):
        total = h_in[j * n_heads].astype(f32)
        for h in range(1, n_heads):
            total = total + h_in[j * n_heads + h].astype(f32)
        hidden_ref[:, j * cols : (j + 1) * cols] = total.astype(jnp.bfloat16)

    drain()

    def sent_row(zb):
        for dx in range(X):
            to_core(zb, lax.rem(x + dx, X)).wait_send()
        for dx in range(1, X):
            to_x(zb, dx).wait_send()
        pl.when(zb < z)(lambda: to_z(zb).wait_send())

    each_row(sent_row)

    def sent(b, carry):
        pl.when((b != me) | (to_head != head))(lambda: to_owner(b).wait_send())
        return carry

    lax.fori_loop(0, n, sent, 0)


def reduce_beacons(n, n_heads, terms, wk, wv):
    _, rows, both = terms.shape
    cols, width = wk.shape
    vmem = pl.BlockSpec(memory_space=pltpu.VMEM)
    low, dma = jnp.bfloat16, pltpu.SemaphoreType.DMA
    sems = spread_sems(n)
    X = 1
    while X * X * 4 <= n // 2:
        X *= 2
    Z, others = n // 2 // X, max(X - 1, 1)
    return pl.pallas_call(
        functools.partial(reduce_kernel, n, n_heads),
        out_shape=(
            jax.ShapeDtypeStruct((rows, both), low),
            jax.ShapeDtypeStruct((rows, cols * (n // n_heads)), low),
        ),
        in_specs=[vmem] * 3,
        out_specs=(vmem, vmem),
        scratch_shapes=[
            pltpu.VMEM((n, rows, both), low),
            pltpu.VMEM((Z * X, rows, both), low),
            pltpu.VMEM((Z, others, rows, both), low),
            pltpu.VMEM((Z, others, rows, both), low),
            pltpu.VMEM((Z, rows, both), low),
            pltpu.VMEM((Z, rows, both), low),
            pltpu.VMEM((Z, rows, both), jnp.float32),
            pltpu.VMEM((n, rows, cols), low),
            pltpu.VMEM((n, rows, cols), low),
        ]
        + sems
        + [dma((2, Z * X)), dma((2, Z, others)), dma((2, Z)), dma((n,)), dma((n,))],
        compiler_params=pltpu.CompilerParams(
            collective_id=1, has_side_effects=True, vmem_limit_bytes=32 * 1024 * 1024
        ),
    )(terms, wk, wv)


def per_device(
    n_heads,
    queries,
    keys,
    values,
    dout,
    beacon_keys,
    beacon_values,
    beacon_key_weight,
    beacon_value_weight,
    lengths,
    counts,
):
    n = lengths.shape[0]
    rows, width = beacon_keys.shape
    gathered = gather_beacons(n, beacon_keys, beacon_values)
    query_grad, key_grad, value_grad, terms = attention(
        queries, keys, values, dout, gathered.reshape(n * rows, 2 * width), lengths, counts
    )
    own, hidden = reduce_beacons(
        n, n_heads, terms.reshape(n, rows, 2 * width), beacon_key_weight, beacon_value_weight
    )
    return (query_grad, key_grad, value_grad, own[:, :width], own[:, width:], hidden)


def solution(mesh):
    spec = P("ctx", "head")
    return jax.shard_map(
        functools.partial(per_device, mesh.shape["head"]),
        mesh=mesh,
        in_specs=(spec,) * 8 + (P(), P()),
        out_specs=(spec,) * 6,
        check_vma=False,
    )
```
